32 devices in a mesh: grp: 2 (over x), blk: 16 (over z, y, core).
Axes of the slice: x: 2, y: 2, z: 4, core: 2. Of those that a mesh axis runs over, the one named last changes fastest.
Arguments:
- features: bfloat16 [4096, 256], P(('grp', 'blk')), may hold values from -6 to 6
- dest: int32 [4096, 1], P(('grp', 'blk')), may hold values from 0 to 15; in each aligned block of 128 rows (0 to 127, 128 to 255, ...) at most 16 rows name the same one
- placement: int32 [32, 256], P(('grp', 'blk')), may hold values from 0 to 255, each once within a row
- weight: bfloat16 [27, 256, 128], replicated, may hold values from -0.078125 to 0.078125
- grad_out: bfloat16 [16, 128, 4, 128], P('grp', 'blk'), may hold values from -6 to 6
Outputs:
- output: bfloat16 [16, 128, 4, 128], P('grp', 'blk')
- grad_rows: bfloat16 [4096, 256], P(('grp', 'blk'))
- weight_grad: bfloat16 [27, 256, 128], replicated
The draws below stay inside these ranges and needn't reach their ends.
Inputs may be any that keep to these rules, and one draw needn't show every extreme that they name: `dest`: among the rows of one device no value is named by more than 16 rows, a bound that some block reaches. `placement`: each row is a permutation of 0 to 255.
All inputs are finite; a program needn't handle non-finite values.
Results may differ from the reference program's by a relative error of at most 0.0013.
Values may be sent and summed in bfloat16 or wider, within the bound.
No kernel may reach another device: no remote copies, remote signals or barrier semaphores. Data moves between devices by JAX's collectives and lax.ppermute only.
A program may use at most 64 MiB of HBM per device.

```python
import math
import jax
import jax.numpy as jnp
import numpy as np
from jax import lax

C = 256
CO = 128
RX = 8
RY = 8
RZ = 4
VOX = 256
CAP = 16
ROWS = 128
TOTAL = 4096
NX = 16
NY = 128
N_GRP = 2
N_BLK = 16
DEVICES = 32


def shard_levels(key, extent, split, low, largest):
    level = 1.0
    for position, shards_of in split:
        draws = jax.random.uniform(jax.random.fold_in(jax.random.fold_in(key, 6), position), (shards_of,), jnp.float32, low / len(split), largest / len(split))
        level = level * jnp.repeat(jnp.exp(draws), extent[position] // shards_of).reshape((-1,) + (1,) * (len(extent) - 1 - position))
    return level


def deal_out(stream_key, own, number, rows, amount, top, reach, lean):
    order = jax.random.permutation(stream_key, amount)
    packed, usual = load_shares(amount, rows * top, reach, lean, True), load_shares(amount, rows * top, reach, lean, False)
    places = jnp.arange(amount)

    def named(tallies, offset_by):
        used = int((tallies > 0).sum())
        fixed = max(1, used // 4)
        shifted = fixed + (places - fixed + offset_by * (used - fixed)) % max(1, amount - fixed)
        return jnp.zeros((amount,), jnp.int32).at[order[jnp.where(places < fixed, places, shifted)]].set(jnp.asarray(tallies, jnp.int32))

    tallies = jnp.where(number % 4 == 0, named(packed, number // 4), named(usual, number - number // 4 - 1))
    mixed = jax.random.permutation(jax.random.fold_in(own, 3), amount)
    giver, sink = mixed[0:amount // 2 * 2:2], mixed[1:amount // 2 * 2:2]
    room = jnp.minimum(tallies[giver] - 1, reach - tallies[sink]) // 2
    room = jnp.where((giver == order[0]) | (sink == order[0]) | (tallies[sink] == 0), 0, jnp.maximum(room, 0))
    shifted = jax.random.randint(jax.random.fold_in(own, 4), (amount // 2,), 0, 1 << 20) % (room + 1)
    tallies = tallies.at[giver].add(-shifted).at[sink].add(shifted)
    items = jnp.searchsorted(jnp.cumsum(tallies), jnp.arange(rows * top), side="right").astype(jnp.int32)
    table = items.reshape(top, rows).T
    table = table[jax.random.permutation(jax.random.fold_in(own, 1), rows)]
    offset_by = jax.random.randint(jax.random.fold_in(own, 2), (rows, 1), 0, top)
    return jnp.take_along_axis(table, (jnp.arange(top)[None, :] + offset_by) % top, axis=1)


def load_shares(count, total, most, slope, full):
    weights = [(1 << 20) // math.isqrt(grade ** slope) + 1 for grade in range(1, count + 1)]
    largest = most if full else min(most, max(-(-total // count), total * weights[0] // sum(weights)))
    least = 1 if total - largest >= count - 1 else 0
    holding, spare = [largest] + [least] * (count - 1), total - largest - least * (count - 1)
    while spare > 0:
        free = [i for i in range(1, count) if holding[i] < largest] or [i for i in range(1, count) if holding[i] < most]
        mass, remaining = sum([weights[i] for i in free]), spare
        for i in free:
            more = min(most - holding[i], max(1, remaining * weights[i] // mass), spare)
            holding[i] = holding[i] + more
            spare = spare - more
    return np.array(holding)


def centred(stream_key, dims, deviation, bound, split=(), kind=jnp.bfloat16):
    level = shard_levels(stream_key, dims, split, -0.22, 0.18) if split else 1.0
    entries = jax.random.normal(stream_key, dims, jnp.float32) * deviation * level
    return jnp.minimum(jnp.maximum(entries, -bound), bound).astype(kind)


def setup_inputs(seed: int = 0) -> dict:
    seeds = jax.random.split(jax.random.key(seed), 6)
    features = centred(seeds[0], (TOTAL, C), 1.0, 6.0, ((0, 32),))
    dest_keys = jax.random.split(jax.random.fold_in(seeds[1], 1), TOTAL // ROWS)
    dest_turns = jax.random.permutation(jax.random.fold_in(seeds[1], 3), TOTAL // ROWS)
    dest = jax.vmap(lambda own, number: deal_out(jax.random.fold_in(seeds[1], 2), own, number, ROWS, N_BLK, 1, CAP, 2))(dest_keys, dest_turns).reshape((TOTAL, 1))
    placement = jax.vmap(lambda own: jax.random.permutation(own, VOX))(jax.random.split(seeds[2], DEVICES)).reshape((DEVICES, VOX)).astype(jnp.int32)
    weight = centred(seeds[3], (27, C, CO), (27 * C) ** -0.5, 0.078125)
    grad_out = centred(seeds[4], (NX, NY, RZ, CO), 1.0, 6.0, ((0, 2), (1, 16)))
    return {"features": features, "dest": dest, "placement": placement, "weight": weight, "grad_out": grad_out}


def reference(features, dest, placement, weight, grad_out):
    devices = N_GRP * N_BLK
    target = dest[:, 0].reshape(devices, ROWS)
    owners = jnp.arange(N_BLK, dtype=jnp.int32)
    one_hot = (target[:, :, None] == owners[None, None, :]).astype(jnp.int32)
    slot_rank = lax.optimization_barrier(jnp.sum((jnp.cumsum(one_hot, axis=1) - one_hot) * one_hot, axis=2))
    sender = jnp.arange(devices, dtype=jnp.int32)[:, None]
    group_index = sender // N_BLK
    block_index = sender % N_BLK
    receiver = group_index * N_BLK + target
    slot_index = block_index * CAP + slot_rank
    voxel = placement[receiver, slot_index]
    pos_x = (group_index * RX + voxel // (RY * RZ)).reshape(-1)
    pos_y = (target * RY + voxel // RZ % RY).reshape(-1)
    pos_z = (voxel % RZ).reshape(-1)
    grid = jnp.zeros((NX, NY, RZ, C), jnp.bfloat16).at[pos_x, pos_y, pos_z].set(features)
    occupied = jnp.zeros((NX, NY, RZ), jnp.float32).at[pos_x, pos_y, pos_z].set(1.0)
    occupied = occupied.reshape(-1, 1)
    count = NX * NY * RZ
    padded = jnp.pad(grid, ((1, 1), (1, 1), (1, 1), (0, 0)))
    total = jnp.zeros((count, CO), jnp.float32)
    for offset in range(27):
        shift_x, shift_y, shift_z = (offset // 9, offset // 3 % 3, offset % 3)
        window = padded[shift_x:shift_x + NX, shift_y:shift_y + NY, shift_z:shift_z + RZ].reshape(count, C)
        total = total + jnp.dot(window, weight[offset], preferred_element_type=jnp.float32)
    output = (total * occupied).astype(jnp.bfloat16).reshape(NX, NY, RZ, CO)
    masked_grad = (grad_out.reshape(count, CO).astype(jnp.float32) * occupied).astype(jnp.bfloat16)
    grad_padded = jnp.pad(masked_grad.reshape(NX, NY, RZ, CO), ((1, 1), (1, 1), (1, 1), (0, 0)))
    back_total = jnp.zeros((count, C), jnp.float32)
    partials = []
    for offset in range(27):
        shift_x, shift_y, shift_z = (offset // 9, offset // 3 % 3, offset % 3)
        window = grad_padded[2 - shift_x:2 - shift_x + NX, 2 - shift_y:2 - shift_y + NY, 2 - shift_z:2 - shift_z + RZ].reshape(count, CO)
        back_total = back_total + lax.dot_general(window, weight[offset], (((1,), (1,)), ((), ())), preferred_element_type=jnp.float32)
        source = padded[shift_x:shift_x + NX, shift_y:shift_y + NY, shift_z:shift_z + RZ].reshape(count, C)
        partials.append(lax.dot_general(source, masked_grad, (((0,), (0,)), ((), ())), preferred_element_type=jnp.float32))
    grad_grid = (back_total * occupied).astype(jnp.bfloat16).reshape(NX, NY, RZ, C)
    grad_scale = 1.0 / math.sqrt(ROWS * N_GRP * N_BLK)
    weight_grad = (jnp.stack(partials) * grad_scale).astype(jnp.bfloat16)
    grad_rows = grad_grid[pos_x, pos_y, pos_z]
    return (output, grad_rows, weight_grad)
```

```python
import functools
import math

import jax
import jax.numpy as jnp
from jax import lax
from jax.experimental import pallas as pl
from jax.experimental.pallas import tpu as pltpu
from jax.sharding import PartitionSpec as P

LANES = 128
F32, BF16, I32 = jnp.float32, jnp.bfloat16, jnp.int32


def iota(shape, axis):
    return lax.broadcasted_iota(I32, shape, axis)


def one_hot(hits):
    return jnp.where(hits, 1.0, 0.0).astype(BF16)


def mm(a, b):
    return lax.dot_general(a, b, (((1,), (0,)), ((), ())), preferred_element_type=F32)


def mm_t(a, b):
    return lax.dot_general(a, b, (((1,), (1,)), ((), ())), preferred_element_type=F32)


def pack_kernel(sizes, cap, features, dest, placement, grad, packed, slots):
    size_x, size_y, size_z = sizes
    rows, channels = features.shape
    voxels = grad.shape[0]
    lane = iota((rows, LANES), 1)
    target = dest[...]
    named = one_hot(lane == target)
    earlier = one_hot(iota((rows, rows), 0) > iota((rows, rows), 1))
    rank = jnp.sum(mm(earlier, named) * named.astype(F32), axis=1, keepdims=True)
    slot = target.astype(F32) * cap + rank
    diagonal = iota((rows, rows), 0) == iota((rows, rows), 1)
    slot_row = jnp.sum(jnp.where(diagonal, slot, 0.0), axis=0, keepdims=True)
    slots[...] = slot_row.astype(I32)
    at = 0
    for c in range(0, channels, LANES):
        packed[at : at + rows, :] = features[:, c : c + LANES]
        at += rows
    row, col = iota((voxels, voxels), 0), iota((voxels, voxels), 1)
    moved = (col % size_z) * (size_x * size_y) + col // size_z
    packed[at : at + voxels, :] = mm(one_hot(row == moved), grad[...]).astype(BF16)
    at += voxels
    spots = placement[...].astype(F32)
    index_rows = [slot_row] + [spots[:, c : c + LANES] for c in range(0, voxels, LANES)]
    index_rows.append(jnp.zeros((16 - len(index_rows), LANES), F32))
    packed[at : at + 16, :] = jnp.concatenate(index_rows, axis=0).astype(BF16)


def scene_kernel(
    dims,
    me_ref,
    where_ref,
    slot_ref,
    packed,
    weight,
    output,
    grad_rows,
    weight_grad,
    slots,
    grid,
    masked,
    masked_t,
    padded_grad,
    padded_grid,
    gathered,
    spots,
    spots_s,
    acc_w,
    acc_o,
    sem,
):
    grp_count, blk_count, cap, rows, channels, size_x, size_y, size_z, scale = dims
    voxels = size_x * size_y * size_z
    out_channels = LANES
    devices = grp_count * blk_count
    nx, ny = grp_count * size_x, blk_count * size_y
    plane = size_x * size_y
    tall = 8
    halves = channels // LANES
    grads_at = halves * rows
    index_at = grads_at + voxels
    my_grp, my_blk = me_ref[0], me_ref[1]

    def fill(s, _):
        at = where_ref[s]
        slot_row = packed[at, index_at : index_at + 16, :].astype(F32)[0:1, :].astype(I32)
        chosen = one_hot(iota((voxels, rows), 0) == slot_row)
        pieces = [packed[at, h * rows : (h + 1) * rows, :] for h in range(halves)]
        pieces.append(jnp.ones((rows, LANES), BF16))
        held = mm(chosen, jnp.concatenate(pieces, axis=1)).astype(BF16)
        g, b = s // blk_count, s % blk_count
        place = pl.ds(pl.multiple_of(b * cap, cap), cap)
        for d in range(blk_count):
            slots[g * blk_count + d, place, :] = held[d * cap : (d + 1) * cap, :]
        return 0

    lax.fori_loop(0, devices, fill, 0)

    padded_grad[...] = jnp.zeros(padded_grad.shape, F32)
    padded_grid[...] = jnp.zeros(padded_grid.shape, F32)

    stretch = one_hot(
        iota((plane * tall, voxels), 0)
        == (iota((plane * tall, voxels), 1) % plane) * tall + iota((plane * tall, voxels), 1) // plane + 1
    )

    def spot_row(r):
        at = where_ref[r]
        block = packed[at, index_at : index_at + 16, :].astype(F32)
        return jnp.concatenate(
            [block[1 + h : 2 + h, :] for h in range(voxels // LANES)], axis=1
        ).astype(I32)

    def place_region(r):
        spot = spot_row(r)
        spots[pl.ds(r, 1), :] = spot
        key = (spot % size_z) * plane + spot // size_z
        chosen = one_hot(iota((voxels, voxels), 0) == key)
        found = mm(chosen, slots[r])
        cells = found[:, :channels]
        occupied = found[:, channels:]
        cotangent = packed[where_ref[r], grads_at : grads_at + voxels, :].astype(F32) * occupied
        g, d = r // blk_count, r % blk_count

        tall_grad = mm(stretch, cotangent.astype(BF16)).reshape(size_x, size_y, tall, out_channels)
        ys = pl.ds(d * size_y + 1, size_y)

        @pl.when(g == my_grp)
        def _():
            padded_grad[1 : size_x + 1, ys] = tall_grad

        @pl.when(g == my_grp - 1)
        def _():
            padded_grad[0:1, ys] = tall_grad[size_x - 1 : size_x]

        @pl.when(g == my_grp + 1)
        def _():
            padded_grad[size_x + 1 : size_x + 2, ys] = tall_grad[0:1]

        shape = (size_z, size_x, size_y, -1)
        return cells.reshape(shape), cotangent.reshape(shape)

    def place_pair(pair, _):
        r = pair * 2
        g, d = r // blk_count, r % blk_count
        cells0, cot0 = place_region(r)
        cells1, cot1 = place_region(r + 1)
        xs = pl.ds(g * size_x, size_x)
        ys = pl.ds(pl.multiple_of(d * size_y, 2 * size_y), 2 * size_y)
        grid[:, xs, ys, :] = jnp.concatenate([cells0, cells1], axis=2).astype(BF16)
        masked[:, xs, ys, :] = jnp.concatenate([cot0, cot1], axis=2).astype(BF16)
        return 0

    lax.fori_loop(0, devices // 2, place_pair, 0)

    copy = pltpu.make_async_copy(spots.at[pl.ds(pl.multiple_of(my_grp * blk_count, blk_count), blk_count)], spots_s, sem)
    copy.start()

    lane = iota((out_channels, ny), 1)
    zero = jnp.zeros((out_channels, ny), F32)

    def turn(n, _):
        z, x = n // nx, n % nx
        block = masked[z, x].astype(F32).T
        back = jnp.where(lane == ny - 1, zero, pltpu.roll(block, ny - 1, 1))
        ahead = jnp.where(lane == 0, zero, pltpu.roll(block, 1, 1))
        cols = pl.ds(pl.multiple_of(x * ny, ny), ny)
        masked_t[z, 0:LANES, cols] = back.astype(BF16)
        masked_t[z, LANES : 2 * LANES, cols] = block.astype(BF16)
        masked_t[z, 2 * LANES : 3 * LANES, cols] = ahead.astype(BF16)
        return 0

    lax.fori_loop(0, size_z * nx, turn, 0)

    for dx in (-1, 0, 1):
        span = nx - abs(dx)
        first = max(0, dx)

        def for_dz(dz1, _, dx=dx, span=span, first=first):
            dz = dz1 - 1
            acc_w[...] = jnp.zeros(acc_w.shape, F32)

            def add(z, _):
                left = masked_t[z - dz, :, (first - dx) * ny : (first - dx + span) * ny]
                right = grid[z, first : first + span].reshape(span * ny, channels)
                acc_w[...] += mm(left, right)
                return 0

            lax.fori_loop(jnp.maximum(0, dz), jnp.minimum(size_z, size_z + dz), add, 0)
            done = (acc_w[...].T * scale).astype(BF16)
            for dy1 in range(3):
                weight_grad[(dx + 1) * 9 + dy1 * 3 + dz1] = done[:, dy1 * LANES : (dy1 + 1) * LANES]
            return 0

        lax.fori_loop(0, 3, for_dz, 0)

    def outer(dx, dy):
        g, d = my_grp + dx, my_blk + dy
        inside = (g >= 0) & (g < grp_count) & (d >= 0) & (d < blk_count)

        @pl.when(inside)
        def _():
            r = g * blk_count + d
            spot = spots[pl.ds(r, 1), :]
            key = (spot // size_z) * tall + spot % size_z + 1
            wide = (1 if dx else size_x) * (1 if dy else size_y) * tall
            t = iota((wide, voxels), 0)
            x0, y0 = (size_x - 1 if dx < 0 else 0), (size_y - 1 if dy < 0 else 0)
            if dy and not dx:
                want = (t // tall) * (size_y * tall) + y0 * tall + t % tall
            else:
                want = t + (x0 * size_y + y0) * tall
            found = mm(one_hot(want == key), slots[r])
            shape = ((1 if dx else size_x), (1 if dy else size_y), tall, channels)
            at_x = {-1: 0, 0: 1, 1: size_x + 1}[dx]
            at_y = {-1: 0, 0: 1, 1: size_y + 1}[dy]
            padded_grid[at_x : at_x + shape[0], at_y : at_y + shape[1]] = found[:, :channels].reshape(shape)
            if dx == 0 and dy == 0:
                acc_o[:, 0:LANES] = found[:, channels:]

    for dx in (-1, 0, 1):
        for dy in (-1, 0, 1):
            outer(dx, dy)
    occupied = acc_o[:, 0:LANES]
    acc_o[...] = jnp.zeros(acc_o.shape, F32)

    def forward(n, _):
        dx, dy = n // 3, n % 3
        window = padded_grid[pl.ds(dx, size_x), pl.ds(dy, size_y)].reshape(plane * tall, channels)
        taps = jnp.concatenate([weight[n * 3 + i] for i in range(3)], axis=1)
        acc_o[...] += mm(window.astype(BF16), taps)
        return 0

    lax.fori_loop(0, 9, forward, 0)
    total = (
        pltpu.roll(acc_o[:, 0:LANES], 1, 0)
        + acc_o[:, LANES : 2 * LANES]
        + pltpu.roll(acc_o[:, 2 * LANES :], plane * tall - 1, 0)
    )
    rounded = (total * occupied).astype(BF16)
    row, col = iota((voxels, plane * tall), 0), iota((voxels, plane * tall), 1)
    squeeze = one_hot(col == (row // size_z) * tall + row % size_z + 1)
    output[...] = mm(squeeze, rounded).astype(BF16)

    copy.wait()

    def gather(i, _):
        slot = slot_ref[0, i]
        d = slot // cap
        v = spots_s[d, my_blk * cap + slot % cap]
        x, y, z = v // (size_y * size_z), d * size_y + v // size_z % size_y, v % size_z
        for n in range(9):
            column = padded_grad[x + 2 - n // 3, y + 2 - n % 3]
            gathered[n, pl.ds(pl.multiple_of(i * tall, tall), tall), :] = pltpu.roll(column, (tall - z) % tall, 0)
        return 0

    lax.fori_loop(0, rows, gather, 0)

    def backward(n, total):
        for dz1 in range(3):
            window = gathered[n, pl.ds(2 - dz1, rows, stride=tall), :].astype(BF16)
            total = total + mm_t(window, weight[n * 3 + dz1])
        return total

    grad_rows[...] = lax.fori_loop(0, 9, backward, jnp.zeros((rows, channels), F32)).astype(BF16)


def exchange_masks(count):
    even = [1 << i for i in range(count.bit_length() - 2, 0, -1)]
    return even, even[1:] + even[:1]


def gather_all(block, count):
    axes = ("grp", "blk")
    even, odd = exchange_masks(count)

    def swap(value, masks):
        pairs = [(i, i ^ masks[i % 2]) for i in range(count)]
        return lax.ppermute(value, axes, pairs)

    held = block[None]
    for step in range(len(even) - 1):
        held = jnp.concatenate([held, swap(held, (even[step], odd[step]))], axis=0)
    last = swap(held, (even[-1], odd[-1]))
    other = swap(held, (1, 1))
    return jnp.concatenate([held, last, other, swap(last, (1, 1))], axis=0)


def positions(count, me):
    even, odd = exchange_masks(count)
    apart = jnp.arange(count, dtype=I32) ^ me

    def along(masks):
        return sum(((apart // mask) % 2) << i for i, mask in enumerate(masks))

    stream = (me + apart) % 2
    return jnp.where(stream == 0, along(even), along(odd)) + (apart % 2) * (count // 2)


def gathered_shards(features, dest, placement, weight, grad_out):
    rows, channels = features.shape
    grp_count, blk_count = lax.axis_size("grp"), lax.axis_size("blk")
    devices = grp_count * blk_count
    size_x, size_y, size_z, out_channels = grad_out.shape
    voxels = size_x * size_y * size_z
    cap = voxels // blk_count
    nx, ny = grp_count * size_x, blk_count * size_y
    packed_rows = channels // LANES * rows + voxels + 16
    vmem = pl.BlockSpec(memory_space=pltpu.VMEM)
    smem = pl.BlockSpec(memory_space=pltpu.SMEM)
    packed, slot = pl.pallas_call(
        functools.partial(pack_kernel, (size_x, size_y, size_z), cap),
        out_shape=(
            jax.ShapeDtypeStruct((packed_rows, LANES), BF16),
            jax.ShapeDtypeStruct((1, rows), I32),
        ),
        in_specs=[vmem] * 4,
        out_specs=(vmem, vmem),
        name="pack",
    )(features, dest, placement, grad_out.reshape(voxels, out_channels))
    everything = gather_all(packed, devices)
    my_grp, my_blk = lax.axis_index("grp"), lax.axis_index("blk")
    me = jnp.stack([my_grp, my_blk]).astype(I32)
    where = positions(devices, (my_grp * blk_count + my_blk).astype(I32))
    scale = 1.0 / math.sqrt(rows * devices)
    dims = (grp_count, blk_count, cap, rows, channels, size_x, size_y, size_z, scale)
    output, grad_rows, weight_grad = pl.pallas_call(
        functools.partial(scene_kernel, dims),
        out_shape=(
            jax.ShapeDtypeStruct((voxels, out_channels), BF16),
            jax.ShapeDtypeStruct((rows, channels), BF16),
            jax.ShapeDtypeStruct(weight.shape, BF16),
        ),
        in_specs=[smem, smem, smem, vmem, vmem],
        out_specs=(vmem, vmem, vmem),
        scratch_shapes=[
            pltpu.VMEM((devices, voxels, channels + LANES), BF16),
            pltpu.VMEM((size_z, nx, ny, channels), BF16),
            pltpu.VMEM((size_z, nx, ny, out_channels), BF16),
            pltpu.VMEM((size_z, 3 * out_channels, nx * ny), BF16),
            pltpu.VMEM((size_x + 2, ny + 2, 8, out_channels), F32),
            pltpu.VMEM((size_x + 2, size_y + 2, 8, channels), F32),
            pltpu.VMEM((9, rows * 8, out_channels), F32),
            pltpu.VMEM((devices, voxels), I32),
            pltpu.SMEM((blk_count, voxels), I32),
            pltpu.VMEM((3 * out_channels, channels), F32),
            pltpu.VMEM((size_x * size_y * 8, 3 * out_channels), F32),
            pltpu.SemaphoreType.DMA,
        ],
        compiler_params=pltpu.CompilerParams(vmem_limit_bytes=56 * 1024 * 1024),
        name="scene",
    )(me, where, slot, everything, weight)
    return output.reshape(grad_out.shape), grad_rows, weight_grad


def extended(cells, sides, width):
    for axis, dim in sides:
        count = lax.axis_size(axis)
        ends = count - 1
        head = lax.slice_in_dim(cells, 0, width, axis=dim)
        tail = lax.slice_in_dim(cells, cells.shape[dim] - width, cells.shape[dim], axis=dim)
        cells = jnp.concatenate(
            [
                lax.ppermute(tail, axis, [(i, (i + 1) % count) for i in range(ends)]),
                cells,
                lax.ppermute(head, axis, [((i + 1) % count, i) for i in range(ends)]),
            ],
            axis=dim,
        )
    return cells


def summed_shards(features, dest, placement, weight, grad_out):
    row_count, channels = features.shape
    blk_count = lax.axis_size("blk")
    grp_count = lax.axis_size("grp")
    voxel_of_slot = placement[0]
    voxel_count = voxel_of_slot.shape[0]
    capacity = voxel_count // blk_count
    size_x, size_y, size_z, out_channels = grad_out.shape
    target = dest[:, 0]
    owners = jnp.arange(blk_count, dtype=jnp.int32)
    one_hot = (target[:, None] == owners[None, :]).astype(jnp.int32)
    slot_rank = jnp.sum((jnp.cumsum(one_hot, axis=0) - one_hot) * one_hot, axis=1)
    send_counts = jnp.sum(one_hot, axis=0).reshape(blk_count, 1)
    slot_index = target * capacity + slot_rank
    outgoing = jnp.zeros((voxel_count, channels), jnp.bfloat16).at[slot_index].set(features)
    incoming, recv_counts = (
        lax.all_to_all(
            outgoing.reshape(blk_count, capacity, channels),
            "blk",
            split_axis=0,
            concat_axis=0,
            tiled=True,
        ),
        lax.all_to_all(send_counts, "blk", split_axis=0, concat_axis=0, tiled=True),
    )
    filled = (
        (jnp.arange(capacity, dtype=jnp.int32)[None, :] < recv_counts)
        .reshape(-1)
        .astype(jnp.float32)
    )
    voxel_rows = (
        jnp.zeros((voxel_count, channels), jnp.bfloat16)
        .at[voxel_of_slot]
        .set(incoming.reshape(voxel_count, channels))
    )
    occupied = jnp.zeros((voxel_count,), jnp.float32).at[voxel_of_slot].set(filled)[:, None]
    voxel_grid = voxel_rows.reshape(size_x, size_y, size_z, channels)
    padded = extended(voxel_grid, (("grp", 0), ("blk", 1)), 1)
    padded = jnp.pad(padded, ((0, 0), (0, 0), (1, 1), (0, 0)))
    shifted = []
    total = jnp.zeros((voxel_count, out_channels), jnp.float32)
    for offset in range(27):
        shift_x, shift_y, shift_z = (offset // 9, offset // 3 % 3, offset % 3)
        window = padded[
            shift_x : shift_x + size_x, shift_y : shift_y + size_y, shift_z : shift_z + size_z
        ].reshape(voxel_count, channels)
        shifted.append(window)
        total = total + jnp.dot(window, weight[offset], preferred_element_type=jnp.float32)
    output = (total * occupied).astype(jnp.bfloat16).reshape(size_x, size_y, size_z, out_channels)
    masked_grad = (
        grad_out.reshape(voxel_count, out_channels).astype(jnp.float32) * occupied
    ).astype(jnp.bfloat16)
    grad_padded = extended(
        masked_grad.reshape(size_x, size_y, size_z, out_channels), (("grp", 0), ("blk", 1)), 1
    )
    grad_padded = jnp.pad(grad_padded, ((0, 0), (0, 0), (1, 1), (0, 0)))
    back_total = jnp.zeros((voxel_count, channels), jnp.float32)
    partials = []
    for offset in range(27):
        shift_x, shift_y, shift_z = (offset // 9, offset // 3 % 3, offset % 3)
        window = grad_padded[
            2 - shift_x : 2 - shift_x + size_x,
            2 - shift_y : 2 - shift_y + size_y,
            2 - shift_z : 2 - shift_z + size_z,
        ].reshape(voxel_count, out_channels)
        back_total = back_total + lax.dot_general(
            window, weight[offset], (((1,), (1,)), ((), ())), preferred_element_type=jnp.float32
        )
        partials.append(
            lax.dot_general(
                shifted[offset],
                masked_grad,
                (((0,), (0,)), ((), ())),
                preferred_element_type=jnp.float32,
            )
        )
    grad_grid = (back_total * occupied).astype(jnp.bfloat16)
    weight_terms = jnp.stack(partials).reshape(27 * channels, out_channels)
    grad_scale = 1.0 / math.sqrt(row_count * blk_count * grp_count)
    weight_grad = (lax.psum(weight_terms, ("grp", "blk")) * grad_scale).astype(jnp.bfloat16)
    weight_grad = weight_grad.reshape(27, channels, out_channels)
    returning = grad_grid[voxel_of_slot].reshape(blk_count, capacity, channels)
    returned = lax.all_to_all(returning, "blk", split_axis=0, concat_axis=0, tiled=True)
    grad_rows = returned.reshape(voxel_count, channels)[slot_index]
    return (output, grad_rows, weight_grad)


def fits(mesh):
    grp_count, blk_count = mesh.shape["grp"], mesh.shape["blk"]
    return grp_count * blk_count <= 64 and blk_count == 16 and grp_count & (grp_count - 1) == 0


def solution(mesh):
    in_specs = (
        P(("grp", "blk"), None),
        P(("grp", "blk"), None),
        P(("grp", "blk"), None),
        P(),
        P("grp", "blk", None, None),
    )
    out_specs = (P("grp", "blk", None, None), P(("grp", "blk"), None), P())
    shards = gathered_shards if fits(mesh) else summed_shards
    return jax.shard_map(shards, mesh=mesh, in_specs=in_specs, out_specs=out_specs, check_vma=False)
```

```python
import functools
import math

import jax
import jax.numpy as jnp
from jax import lax
from jax.experimental import pallas as pl
from jax.experimental.pallas import tpu as pltpu
from jax.sharding import PartitionSpec as P

LANES = 128
TALL = 8
F32, BF16, I32 = jnp.float32, jnp.bfloat16, jnp.int32


def iota(shape, axis):
    return lax.broadcasted_iota(I32, shape, axis)


def one_hot(hits):
    return jnp.where(hits, 1.0, 0.0).astype(BF16)


def rows_at(count, key):
    shape = (count, key.shape[1])
    places = iota(shape, 0).astype(BF16)
    return jnp.where(places == jnp.broadcast_to(key.astype(BF16), shape), 1.0, 0.0).astype(BF16)


def mm(a, b):
    return lax.dot_general(a, b, (((1,), (0,)), ((), ())), preferred_element_type=F32)


def mm_t(a, b):
    return lax.dot_general(a, b, (((1,), (1,)), ((), ())), preferred_element_type=F32)


def half_order(z, flat, group, plane):
    return z // 2 * (2 * plane) + (z + group) % 2 * plane + flat


def pack_kernel(sizes, cap, dest, placement, grad, packed, slots):
    size_x, size_y, size_z = sizes
    rows = dest.shape[1]
    voxels = grad.shape[0]
    plane = size_x * size_y
    lane = iota((rows, LANES), 1)
    upright = iota((rows, rows), 0) == iota((rows, rows), 1)
    target = jnp.sum(jnp.where(upright, dest[...], 0), axis=1, keepdims=True)
    named = one_hot(lane == target)
    earlier = one_hot(iota((rows, rows), 0) > iota((rows, rows), 1))
    rank = jnp.sum(mm(earlier, named) * named.astype(F32), axis=1, keepdims=True)
    slot = target.astype(F32) * cap + rank
    slot_row = jnp.sum(jnp.where(upright, slot, 0.0), axis=0, keepdims=True)
    counts = jnp.sum(named.astype(F32), axis=0, keepdims=True)
    slots[...] = slot_row.astype(I32)
    row, col = iota((voxels, voxels), 0), iota((voxels, voxels), 1)
    moved = half_order(row % size_z, row // size_z, lax.axis_index("grp"), plane)
    turned = mm(grad[...].astype(F32).T.astype(BF16), one_hot(col == moved)).astype(BF16)
    halves = voxels // LANES
    for h in range(halves):
        packed[h * LANES : (h + 1) * LANES, :] = turned[:, h * LANES : (h + 1) * LANES]
    spots = placement[...].astype(F32)
    index_rows = [slot_row, counts] + [spots[:, h * LANES : (h + 1) * LANES] for h in range(halves)]
    index_rows.append(jnp.zeros((16 - len(index_rows), LANES), F32))
    packed[halves * LANES : halves * LANES + 16, :] = jnp.concatenate(index_rows, axis=0).astype(BF16)


def source(me, buffer, t, count):
    even, odd = exchange_masks(count)

    def apart(masks):
        total = masks[-1] * (buffer % 2)
        for i in range(len(masks) - 1):
            total = total + (t >> i) % 2 * masks[i]
        return total

    holder = me ^ (buffer // 2)
    return holder ^ jnp.where(holder % 2 == 0, apart(even), apart(odd))


def cotangent_kernel(
    dims,
    slot_ref,
    block0,
    block1,
    block2,
    block3,
    weight,
    grad_rows,
    tiles,
    slot_rows,
    spots,
    filled,
    padded,
    gathered,
    stretch,
    counts,
    occupied,
    masked,
    spots_s,
    sem,
):
    grp_count, blk_count, cap, rows, channels, size_x, size_y, size_z = dims
    voxels = size_x * size_y * size_z
    devices = grp_count * blk_count
    plane = size_x * size_y
    halves = voxels // LANES
    blocks = (block0, block1, block2, block3)
    each = devices // 4
    my_grp, my_blk = lax.axis_index("grp"), lax.axis_index("blk")
    me = my_grp * blk_count + my_blk

    for k, block in enumerate(blocks):

        def read(t, _, k=k, block=block):
            s = source(me, k, t, devices)
            index = block[t, halves * LANES : halves * LANES + 16, :].astype(F32)
            slot_rows[pl.ds(s, 1), :] = index[0:1].astype(I32)
            counts[pl.ds(s, 1), :] = index[1:2]
            row = jnp.concatenate([index[2 + h : 3 + h] for h in range(halves)], axis=1)
            spots[pl.ds(s, 1), :] = row.astype(I32)
            return 0

        lax.fori_loop(0, each, read, 0)
    copy = pltpu.make_async_copy(
        spots.at[pl.ds(pl.multiple_of(my_grp * blk_count, blk_count), blk_count)], spots_s, sem
    )
    copy.start()

    spread = one_hot(iota((blk_count, voxels), 0) == iota((blk_count, voxels), 1) // cap)
    rank = (iota((blk_count, voxels), 1) % cap).astype(F32)
    for g in range(grp_count):
        sent = counts[g * blk_count : (g + 1) * blk_count, :].T[:blk_count].astype(BF16)
        held = jnp.where(rank < mm(sent, spread), 1.0, 0.0)
        filled[g * blk_count : (g + 1) * blk_count, :] = held
        row, col = iota((plane * TALL, voxels), 0), iota((plane * TALL, voxels), 1)
        z = row % TALL - 1
        inside = (z >= 0) & (z < size_z)
        stretch[g] = one_hot(inside & (col == half_order(z, row // TALL, g, plane)))

    zero_plane = jnp.zeros((1,) + padded.shape[1:], F32)
    zero_line = jnp.zeros((padded.shape[0], 1) + padded.shape[2:], F32)

    @pl.when(my_grp == 0)
    def _():
        padded[0:1] = zero_plane

    @pl.when(my_grp == grp_count - 1)
    def _():
        padded[size_x + 1 : size_x + 2] = zero_plane

    padded[:, 0:1] = zero_line
    padded[:, padded.shape[1] - 1 :] = zero_line
    for z in range(size_z):
        tiles[z, :, 0:LANES] = jnp.zeros((LANES, LANES), BF16)
        tiles[z, :, (blk_count + 1) * LANES :] = jnp.zeros((LANES, LANES), BF16)

    def occupy(r, _):
        spot = spots[pl.ds(r, 1), :]
        key = half_order(spot % size_z, spot // size_z, r // blk_count, plane)
        held = jnp.broadcast_to(filled[pl.ds(r, 1), :], (16, voxels)).astype(BF16)
        occupied[pl.ds(r, 1), :] = mm_t(held, rows_at(voxels, key))[0:1]
        return 0

    lax.fori_loop(0, devices, occupy, 0, unroll=8)

    for k, block in enumerate(blocks):

        def mask(t, _, k=k, block=block):
            r = source(me, k, t, devices)
            there = occupied[pl.ds(r, 1), :].astype(BF16)
            for h in range(halves):
                at = slice(h * LANES, (h + 1) * LANES)
                masked[r, :, at] = block[t, at, :] * there[:, at]
            return 0

        lax.fori_loop(0, each, mask, 0, unroll=4)

    first = iota((LANES, LANES), 1) < plane

    def tile(d, _):
        cols = pl.ds(pl.multiple_of((d + 1) * LANES, LANES), LANES)
        for h in range(halves):
            at = slice(h * LANES, (h + 1) * LANES)
            left, right = masked[d, :, at], masked[blk_count + d, :, at]
            tiles[2 * h, :, cols] = jnp.where(first, left, right)
            tiles[2 * h + 1, :, cols] = pltpu.roll(jnp.where(first, right, left), plane, 1)
        return 0

    lax.fori_loop(0, blk_count, tile, 0, unroll=4)

    def stand(d, _):
        found = mm_t(stretch[my_grp], masked[my_grp * blk_count + d])
        padded[1 : size_x + 1, pl.ds(d * size_y + 1, size_y)] = found.reshape(size_x, size_y, TALL, LANES)
        return 0

    lax.fori_loop(0, blk_count, stand, 0, unroll=2)

    near = 1 - my_grp
    lines = pl.ds(pl.multiple_of(jnp.where(my_grp == 0, 0, size_x - 1) * size_y * TALL, size_y * TALL), size_y * TALL)

    def stand_near(d, _):
        found = mm_t(stretch[near, lines, :], masked[near * blk_count + d])
        at_x = pl.ds(jnp.where(my_grp == 0, size_x + 1, 0), 1)
        padded[at_x, pl.ds(d * size_y + 1, size_y)] = found.reshape(1, size_y, TALL, LANES)
        return 0

    lax.fori_loop(0, blk_count, stand_near, 0, unroll=4)

    copy.wait()
    sub = iota((TALL, LANES), 0)

    def gather(group, _):
        found = [jnp.zeros((TALL, LANES), F32)] * 27
        for j in range(TALL):
            slot = slot_ref[0, group * TALL + j]
            d = slot // cap
            v = spots_s[d, my_blk * cap + slot % cap]
            x, y, z = v // (size_y * size_z), d * size_y + v // size_z % size_y, v % size_z
            for n in range(27):
                line = padded[x + 2 - n // 9, y + 2 - n // 3 % 3, pl.ds(z + 2 - n % 3, 1), :]
                found[n] = jnp.where(sub == j, jnp.broadcast_to(line, (TALL, LANES)), found[n])
        for n in range(27):
            gathered[n, pl.ds(pl.multiple_of(group * TALL, TALL), TALL), :] = found[n]
        return 0

    lax.fori_loop(0, rows // TALL, gather, 0)

    def backward(n, total):
        windows = jnp.concatenate([gathered[n * 3 + i] for i in range(3)], axis=1).astype(BF16)
        taps = jnp.concatenate([weight[n * 3 + i] for i in range(3)], axis=1)
        return total + mm_t(windows, taps)

    grad_rows[...] = lax.fori_loop(0, 9, backward, jnp.zeros((rows, channels), F32), unroll=3).astype(BF16)


def scene_kernel(
    dims,
    block0,
    block1,
    block2,
    block3,
    weight,
    tiles,
    slot_rows,
    spots,
    filled,
    output,
    weight_grad,
    slots,
    grid,
    shifted,
    padded,
    acc_w,
    acc_o,
):
    grp_count, blk_count, cap, rows, channels, size_x, size_y, size_z, scale = dims
    voxels = size_x * size_y * size_z
    devices = grp_count * blk_count
    plane = size_x * size_y
    blocks = (block0, block1, block2, block3)
    each = devices // 4
    my_grp, my_blk = lax.axis_index("grp"), lax.axis_index("blk")
    me = my_grp * blk_count + my_blk
    half = me % 2

    for k, block in enumerate(blocks):

        def fill(t, _, k=k, block=block):
            s = source(me, k, t, devices)
            chosen = rows_at(voxels, slot_rows[pl.ds(s, 1), :])
            held = mm(chosen, block[t]).astype(BF16)
            g, b = s // blk_count, s % blk_count
            place = pl.ds(pl.multiple_of(b * cap, cap), cap)
            for d in range(blk_count):
                slots[g * blk_count + d, place, :] = held[d * cap : (d + 1) * cap, :]
            return 0

        lax.fori_loop(0, each, fill, 0, unroll=4)

    def place_region(r, _):
        spot = spots[pl.ds(r, 1), :]
        key = spot % size_z * plane + spot // size_z
        found = mm(rows_at(voxels, key), slots[r]).astype(BF16)
        at = r % blk_count * LANES + r // blk_count * plane
        for z in range(size_z):
            grid[z, pl.ds(pl.multiple_of(at, plane), plane), :] = found[z * plane : (z + 1) * plane]
        return 0

    lax.fori_loop(0, devices, place_region, 0, unroll=4)

    def outer(dx, dy):
        g, d = my_grp + dx, my_blk + dy
        inside = (g >= 0) & (g < grp_count) & (d >= 0) & (d < blk_count)
        shape = ((1 if dx else size_x), (1 if dy else size_y), TALL, channels)
        at_x = {-1: 0, 0: 1, 1: size_x + 1}[dx]
        at_y = {-1: 0, 0: 1, 1: size_y + 1}[dy]
        there = (slice(at_x, at_x + shape[0]), slice(at_y, at_y + shape[1]))

        @pl.when(inside)
        def _():
            r = g * blk_count + d
            spot = spots[pl.ds(r, 1), :]
            key = spot // size_z * TALL + spot % size_z + 1
            t = iota((shape[0] * shape[1] * TALL, voxels), 0)
            x0, y0 = (size_x - 1 if dx < 0 else 0), (size_y - 1 if dy < 0 else 0)
            if dy and not dx:
                want = t // TALL * (size_y * TALL) + y0 * TALL + t % TALL
            else:
                want = t + (x0 * size_y + y0) * TALL
            padded[there] = mm(one_hot(want == key), slots[r]).reshape(shape)

        @pl.when(jnp.logical_not(inside))
        def _():
            padded[there] = jnp.zeros(shape, F32)

    for dx in (-1, 0, 1):
        for dy in (-1, 0, 1):
            outer(dx, dy)

    acc_o[...] = jnp.zeros(acc_o.shape, F32)

    def forward(n, _):
        dx, dy = n // 3, n % 3
        window = padded[pl.ds(dx, size_x), pl.ds(dy, size_y)].reshape(plane * TALL, channels)
        taps = jnp.concatenate([weight[n * 3 + i] for i in range(3)], axis=1)
        acc_o[...] += mm(window.astype(BF16), taps)
        return 0

    lax.fori_loop(0, 9, forward, 0)
    spot = spots[pl.ds(me, 1), :]
    key = jnp.where(filled[pl.ds(me, 1), :] > 0, spot // size_z * TALL + spot % size_z + 1, -1)
    occupied = mm(one_hot(iota((plane * TALL, voxels), 0) == key), jnp.ones((voxels, LANES), BF16))
    total = (
        pltpu.roll(acc_o[:, 0:LANES], 1, 0)
        + acc_o[:, LANES : 2 * LANES]
        + pltpu.roll(acc_o[:, 2 * LANES :], plane * TALL - 1, 0)
    )
    rounded = (total * occupied).astype(BF16)
    row, col = iota((voxels, plane * TALL), 0), iota((voxels, plane * TALL), 1)
    squeeze = one_hot(col == row // size_z * TALL + row % size_z + 1)
    output[...] = mm(squeeze, rounded).astype(BF16)

    acc_w[...] = jnp.zeros(acc_w.shape, F32)
    lane = iota((LANES, LANES), 1)
    x, y = lane // size_y, lane % size_y
    nx = grp_count * size_x
    zero = jnp.zeros((LANES, LANES), BF16)

    def for_z(z, _):
        for own_half in range(2):

            def shift(d, _, own_half=own_half):
                def tile(offset):
                    return tiles[z, :, pl.ds(pl.multiple_of((d + 1 + offset) * LANES, LANES), LANES)]

                cols = pl.ds(pl.multiple_of(d * LANES, LANES), LANES)
                beside = {dy: tile(-dy) for dy in (-1, 0, 1)}
                for n in range(5):
                    place = n + 4 * own_half
                    dx, dy = place // 3 - 1, place % 3 - 1
                    ahead = dx * size_y + dy
                    value = beside[0]
                    if ahead:
                        value = pltpu.roll(value, ahead % LANES, 1)
                    if dy:
                        crossing = y == (0 if dy > 0 else size_y - 1)
                        value = jnp.where(crossing, pltpu.roll(beside[dy], (ahead - dy * size_y) % LANES, 1), value)
                    if dx:
                        value = jnp.where((x - dx >= 0) & (x - dx < nx), value, zero)
                    shifted[n * LANES : (n + 1) * LANES, cols] = value
                return 0

            @pl.when(half == own_half)
            def _(shift=shift):
                lax.fori_loop(0, blk_count, shift, 0, unroll=2)

        def add(dz1, _):
            acc_w[dz1] += mm(shifted[...], grid[z + dz1 - 1])
            return 0

        lax.fori_loop(jnp.where(z == 0, 1, 0), jnp.where(z == size_z - 1, 2, 3), add, 0)
        return 0

    lax.fori_loop(0, size_z, for_z, 0)

    def finish(dz1, _):
        done = (acc_w[dz1].T * scale).astype(BF16)
        for n in range(5):
            weight_grad[n * 3 + dz1] = done[:, n * LANES : (n + 1) * LANES]
        return 0

    lax.fori_loop(0, 3, finish, 0)


def exchange_masks(count):
    even = [1 << i for i in range(count.bit_length() - 2, 0, -1)]
    return even, even[1:] + even[:1]


def swap(value, count, masks):
    pairs = [(i, i ^ masks[i % 2]) for i in range(count)]
    return lax.ppermute(value, ("grp", "blk"), pairs)


def gather_all(block, count):
    even, odd = exchange_masks(count)
    held = block[None]
    for step in range(len(even) - 1):
        held = jnp.concatenate([held, swap(held, count, (even[step], odd[step]))], axis=0)
    last = swap(held, count, (even[-1], odd[-1]))
    return held, last, swap(held, count, (1, 1)), swap(last, count, (1, 1))


def gathered_shards(features, dest, placement, weight, grad_out):
    rows, channels = features.shape
    grp_count, blk_count = lax.axis_size("grp"), lax.axis_size("blk")
    devices = grp_count * blk_count
    size_x, size_y, size_z, out_channels = grad_out.shape
    sizes = (size_x, size_y, size_z)
    voxels = size_x * size_y * size_z
    plane = size_x * size_y
    cap = voxels // blk_count
    vmem = pl.BlockSpec(memory_space=pltpu.VMEM)
    smem = pl.BlockSpec(memory_space=pltpu.SMEM)
    packed, slot = pl.pallas_call(
        functools.partial(pack_kernel, sizes, cap),
        out_shape=(
            jax.ShapeDtypeStruct((voxels + 16, LANES), BF16),
            jax.ShapeDtypeStruct((1, rows), I32),
        ),
        in_specs=[vmem] * 3,
        out_specs=(vmem, vmem),
        name="pack",
    )(dest.reshape(1, rows), placement, grad_out.reshape(voxels, out_channels))
    cotangents = gather_all(packed, devices)
    cells = gather_all(features, devices)
    dims = (grp_count, blk_count, cap, rows, channels) + sizes
    grad_rows, tiles, slot_rows, spots, filled = pl.pallas_call(
        functools.partial(cotangent_kernel, dims),
        out_shape=(
            jax.ShapeDtypeStruct((rows, channels), BF16),
            jax.ShapeDtypeStruct((size_z, out_channels, (blk_count + 2) * LANES), BF16),
            jax.ShapeDtypeStruct((devices, rows), I32),
            jax.ShapeDtypeStruct((devices, voxels), I32),
            jax.ShapeDtypeStruct((devices, voxels), F32),
        ),
        in_specs=[smem] + [vmem] * 5,
        out_specs=(vmem,) * 5,
        scratch_shapes=[
            pltpu.VMEM((size_x + 2, blk_count * size_y + 2, TALL, out_channels), F32),
            pltpu.VMEM((27, rows, out_channels), F32),
            pltpu.VMEM((grp_count, plane * TALL, voxels), BF16),
            pltpu.VMEM((devices, LANES), F32),
            pltpu.VMEM((devices, voxels), F32),
            pltpu.VMEM((devices, out_channels, voxels), BF16),
            pltpu.SMEM((blk_count, voxels), I32),
            pltpu.SemaphoreType.DMA,
        ],
        compiler_params=pltpu.CompilerParams(vmem_limit_bytes=28 * 1024 * 1024),
        name="cotangent",
    )(slot, *cotangents, weight)
    scale = 1.0 / math.sqrt(rows * devices)
    output, some = pl.pallas_call(
        functools.partial(scene_kernel, dims + (scale,)),
        out_shape=(
            jax.ShapeDtypeStruct((voxels, out_channels), BF16),
            jax.ShapeDtypeStruct((15, channels, out_channels), BF16),
        ),
        in_specs=[vmem] * 9,
        out_specs=(vmem, vmem),
        scratch_shapes=[
            pltpu.VMEM((devices, voxels, channels), BF16),
            pltpu.VMEM((size_z, blk_count * LANES, channels), BF16),
            pltpu.VMEM((5 * out_channels, blk_count * LANES), BF16),
            pltpu.VMEM((size_x + 2, size_y + 2, TALL, channels), F32),
            pltpu.VMEM((3, 5 * out_channels, channels), F32),
            pltpu.VMEM((plane * TALL, 3 * out_channels), F32),
        ],
        compiler_params=pltpu.CompilerParams(vmem_limit_bytes=36 * 1024 * 1024),
        name="scene",
    )(*cells, weight, tiles, slot_rows, spots, filled)
    odd = lax.axis_index("blk") % 2
    sent = lax.dynamic_slice_in_dim(some, 3 * odd, 12, axis=0)
    received = swap(sent, devices, (1, 1))
    weight_grad = jnp.where(
        odd == 0,
        jnp.concatenate([some, received], axis=0),
        jnp.concatenate([received, some], axis=0),
    )
    return output.reshape(grad_out.shape), grad_rows, weight_grad


def extended(cells, sides, width):
    for axis, dim in sides:
        count = lax.axis_size(axis)
        ends = count - 1
        head = lax.slice_in_dim(cells, 0, width, axis=dim)
        tail = lax.slice_in_dim(cells, cells.shape[dim] - width, cells.shape[dim], axis=dim)
        cells = jnp.concatenate(
            [
                lax.ppermute(tail, axis, [(i, (i + 1) % count) for i in range(ends)]),
                cells,
                lax.ppermute(head, axis, [((i + 1) % count, i) for i in range(ends)]),
            ],
            axis=dim,
        )
    return cells


def summed_shards(features, dest, placement, weight, grad_out):
    row_count, channels = features.shape
    blk_count = lax.axis_size("blk")
    grp_count = lax.axis_size("grp")
    voxel_of_slot = placement[0]
    voxel_count = voxel_of_slot.shape[0]
    capacity = voxel_count // blk_count
    size_x, size_y, size_z, out_channels = grad_out.shape
    target = dest[:, 0]
    owners = jnp.arange(blk_count, dtype=jnp.int32)
    one_hot = (target[:, None] == owners[None, :]).astype(jnp.int32)
    slot_rank = jnp.sum((jnp.cumsum(one_hot, axis=0) - one_hot) * one_hot, axis=1)
    send_counts = jnp.sum(one_hot, axis=0).reshape(blk_count, 1)
    slot_index = target * capacity + slot_rank
    outgoing = jnp.zeros((voxel_count, channels), jnp.bfloat16).at[slot_index].set(features)
    incoming, recv_counts = (
        lax.all_to_all(
            outgoing.reshape(blk_count, capacity, channels),
            "blk",
            split_axis=0,
            concat_axis=0,
            tiled=True,
        ),
        lax.all_to_all(send_counts, "blk", split_axis=0, concat_axis=0, tiled=True),
    )
    filled = (
        (jnp.arange(capacity, dtype=jnp.int32)[None, :] < recv_counts)
        .reshape(-1)
        .astype(jnp.float32)
    )
    voxel_rows = (
        jnp.zeros((voxel_count, channels), jnp.bfloat16)
        .at[voxel_of_slot]
        .set(incoming.reshape(voxel_count, channels))
    )
    occupied = jnp.zeros((voxel_count,), jnp.float32).at[voxel_of_slot].set(filled)[:, None]
    voxel_grid = voxel_rows.reshape(size_x, size_y, size_z, channels)
    padded = extended(voxel_grid, (("grp", 0), ("blk", 1)), 1)
    padded = jnp.pad(padded, ((0, 0), (0, 0), (1, 1), (0, 0)))
    shifted = []
    total = jnp.zeros((voxel_count, out_channels), jnp.float32)
    for offset in range(27):
        shift_x, shift_y, shift_z = (offset // 9, offset // 3 % 3, offset % 3)
        window = padded[
            shift_x : shift_x + size_x, shift_y : shift_y + size_y, shift_z : shift_z + size_z
        ].reshape(voxel_count, channels)
        shifted.append(window)
        total = total + jnp.dot(window, weight[offset], preferred_element_type=jnp.float32)
    output = (total * occupied).astype(jnp.bfloat16).reshape(size_x, size_y, size_z, out_channels)
    masked_grad = (
        grad_out.reshape(voxel_count, out_channels).astype(jnp.float32) * occupied
    ).astype(jnp.bfloat16)
    grad_padded = extended(
        masked_grad.reshape(size_x, size_y, size_z, out_channels), (("grp", 0), ("blk", 1)), 1
    )
    grad_padded = jnp.pad(grad_padded, ((0, 0), (0, 0), (1, 1), (0, 0)))
    back_total = jnp.zeros((voxel_count, channels), jnp.float32)
    partials = []
    for offset in range(27):
        shift_x, shift_y, shift_z = (offset // 9, offset // 3 % 3, offset % 3)
        window = grad_padded[
            2 - shift_x : 2 - shift_x + size_x,
            2 - shift_y : 2 - shift_y + size_y,
            2 - shift_z : 2 - shift_z + size_z,
        ].reshape(voxel_count, out_channels)
        back_total = back_total + lax.dot_general(
            window, weight[offset], (((1,), (1,)), ((), ())), preferred_element_type=jnp.float32
        )
        partials.append(
            lax.dot_general(
                shifted[offset],
                masked_grad,
                (((0,), (0,)), ((), ())),
                preferred_element_type=jnp.float32,
            )
        )
    grad_grid = (back_total * occupied).astype(jnp.bfloat16)
    weight_terms = jnp.stack(partials).reshape(27 * channels, out_channels)
    grad_scale = 1.0 / math.sqrt(row_count * blk_count * grp_count)
    weight_grad = (lax.psum(weight_terms, ("grp", "blk")) * grad_scale).astype(jnp.bfloat16)
    weight_grad = weight_grad.reshape(27, channels, out_channels)
    returning = grad_grid[voxel_of_slot].reshape(blk_count, capacity, channels)
    returned = lax.all_to_all(returning, "blk", split_axis=0, concat_axis=0, tiled=True)
    grad_rows = returned.reshape(voxel_count, channels)[slot_index]
    return (output, grad_rows, weight_grad)


def fits(mesh):
    grp_count, blk_count = mesh.shape["grp"], mesh.shape["blk"]
    return blk_count == 16 and grp_count == 2


def solution(mesh):
    in_specs = (
        P(("grp", "blk"), None),
        P(("grp", "blk"), None),
        P(("grp", "blk"), None),
        P(),
        P("grp", "blk", None, None),
    )
    out_specs = (P("grp", "blk", None, None), P(("grp", "blk"), None), P())
    shards = gathered_shards if fits(mesh) else summed_shards
    return jax.shard_map(shards, mesh=mesh, in_specs=in_specs, out_specs=out_specs, check_vma=False)
```

```python
import functools
import math

import jax
import jax.numpy as jnp
from jax import lax
from jax.experimental import pallas as pl
from jax.experimental.pallas import tpu as pltpu
from jax.sharding import PartitionSpec as P

LANES = 128
TALL = 8
F32, BF16, I32 = jnp.float32, jnp.bfloat16, jnp.int32


def iota(shape, axis):
    return lax.broadcasted_iota(I32, shape, axis)


def one_hot(hits):
    return jnp.where(hits, 1.0, 0.0).astype(BF16)


def rows_at(count, key):
    shape = (count, key.shape[1])
    places = iota(shape, 0).astype(BF16)
    return jnp.where(places == jnp.broadcast_to(key.astype(BF16), shape), 1.0, 0.0).astype(BF16)


def mm(a, b):
    return lax.dot_general(a, b, (((1,), (0,)), ((), ())), preferred_element_type=F32)


def mm_t(a, b):
    return lax.dot_general(a, b, (((1,), (1,)), ((), ())), preferred_element_type=F32)


def half_order(z, flat, group, plane):
    return z // 2 * (2 * plane) + (z + group) % 2 * plane + flat


def pack_kernel(sizes, cap, dest, placement, grad, packed, slots):
    size_x, size_y, size_z = sizes
    rows = dest.shape[1]
    voxels = grad.shape[0]
    plane = size_x * size_y
    lane = iota((rows, LANES), 1)
    upright = iota((rows, rows), 0) == iota((rows, rows), 1)
    target = jnp.sum(jnp.where(upright, dest[...], 0), axis=1, keepdims=True)
    named = one_hot(lane == target)
    earlier = one_hot(iota((rows, rows), 0) > iota((rows, rows), 1))
    rank = jnp.sum(mm(earlier, named) * named.astype(F32), axis=1, keepdims=True)
    slot = target.astype(F32) * cap + rank
    slot_row = jnp.sum(jnp.where(upright, slot, 0.0), axis=0, keepdims=True)
    counts = jnp.sum(named.astype(F32), axis=0, keepdims=True)
    slots[...] = slot_row.astype(I32)
    row, col = iota((voxels, voxels), 0), iota((voxels, voxels), 1)
    moved = half_order(row % size_z, row // size_z, lax.axis_index("grp"), plane)
    turned = mm(grad[...].astype(F32).T.astype(BF16), one_hot(col == moved)).astype(BF16)
    halves = voxels // LANES
    for h in range(halves):
        packed[h * LANES : (h + 1) * LANES, :] = turned[:, h * LANES : (h + 1) * LANES]
    spots = placement[...].astype(F32)
    index_rows = [slot_row, counts] + [spots[:, h * LANES : (h + 1) * LANES] for h in range(halves)]
    index_rows.append(jnp.zeros((16 - len(index_rows), LANES), F32))
    packed[halves * LANES : halves * LANES + 16, :] = jnp.concatenate(index_rows, axis=0).astype(BF16)


def source(me, buffer, t, count):
    even, odd = exchange_masks(count)

    def apart(masks):
        total = masks[-1] * (buffer % 2)
        for i in range(len(masks) - 1):
            total = total + (t >> i) % 2 * masks[i]
        return total

    holder = me ^ (buffer // 2)
    return holder ^ jnp.where(holder % 2 == 0, apart(even), apart(odd))


def cotangent_kernel(
    dims,
    slot_ref,
    block0,
    block1,
    block2,
    block3,
    weight,
    grad_rows,
    tiles,
    slot_rows,
    spots,
    filled,
    padded,
    gathered,
    stretch,
    counts,
    occupied,
    masked,
    spots_s,
    sem,
):
    grp_count, blk_count, cap, rows, channels, size_x, size_y, size_z = dims
    voxels = size_x * size_y * size_z
    devices = grp_count * blk_count
    plane = size_x * size_y
    halves = voxels // LANES
    blocks = (block0, block1, block2, block3)
    each = devices // 4
    my_grp, my_blk = lax.axis_index("grp"), lax.axis_index("blk")
    me = my_grp * blk_count + my_blk

    for k, block in enumerate(blocks):

        def read(t, _, k=k, block=block):
            s = source(me, k, t, devices)
            index = block[t, halves * LANES : halves * LANES + 16, :].astype(F32)
            slot_rows[pl.ds(s, 1), :] = index[0:1].astype(I32)
            counts[pl.ds(s, 1), :] = index[1:2]
            row = jnp.concatenate([index[2 + h : 3 + h] for h in range(halves)], axis=1)
            spots[pl.ds(s, 1), :] = row.astype(I32)
            return 0

        lax.fori_loop(0, each, read, 0)
    copy = pltpu.make_async_copy(
        spots.at[pl.ds(pl.multiple_of(my_grp * blk_count, blk_count), blk_count)], spots_s, sem
    )
    copy.start()

    spread = one_hot(iota((blk_count, voxels), 0) == iota((blk_count, voxels), 1) // cap)
    rank = (iota((blk_count, voxels), 1) % cap).astype(F32)
    for g in range(grp_count):
        sent = counts[g * blk_count : (g + 1) * blk_count, :].T[:blk_count].astype(BF16)
        held = jnp.where(rank < mm(sent, spread), 1.0, 0.0)
        filled[g * blk_count : (g + 1) * blk_count, :] = held
        row, col = iota((plane * TALL, voxels), 0), iota((plane * TALL, voxels), 1)
        z = row % TALL - 1
        inside = (z >= 0) & (z < size_z)
        stretch[g] = one_hot(inside & (col == half_order(z, row // TALL, g, plane)))

    zero_plane = jnp.zeros((1,) + padded.shape[1:], F32)
    zero_line = jnp.zeros((padded.shape[0], 1) + padded.shape[2:], F32)

    @pl.when(my_grp == 0)
    def _():
        padded[0:1] = zero_plane

    @pl.when(my_grp == grp_count - 1)
    def _():
        padded[size_x + 1 : size_x + 2] = zero_plane

    padded[:, 0:1] = zero_line
    padded[:, padded.shape[1] - 1 :] = zero_line
    for z in range(size_z):
        tiles[z, :, 0:LANES] = jnp.zeros((LANES, LANES), BF16)
        tiles[z, :, (blk_count + 1) * LANES :] = jnp.zeros((LANES, LANES), BF16)

    def occupy(r, _):
        spot = spots[pl.ds(r, 1), :]
        key = half_order(spot % size_z, spot // size_z, r // blk_count, plane)
        held = jnp.broadcast_to(filled[pl.ds(r, 1), :], (16, voxels)).astype(BF16)
        occupied[pl.ds(r, 1), :] = mm_t(held, rows_at(voxels, key))[0:1]
        return 0

    lax.fori_loop(0, devices, occupy, 0, unroll=8)

    for k, block in enumerate(blocks):

        def mask(t, _, k=k, block=block):
            r = source(me, k, t, devices)
            there = occupied[pl.ds(r, 1), :].astype(BF16)
            for h in range(halves):
                at = slice(h * LANES, (h + 1) * LANES)
                masked[r, :, at] = block[t, at, :] * there[:, at]
            return 0

        lax.fori_loop(0, each, mask, 0, unroll=4)

    first = iota((LANES, LANES), 1) < plane

    def tile(d, _):
        cols = pl.ds(pl.multiple_of((d + 1) * LANES, LANES), LANES)
        for h in range(halves):
            at = slice(h * LANES, (h + 1) * LANES)
            left, right = masked[d, :, at], masked[blk_count + d, :, at]
            tiles[2 * h, :, cols] = jnp.where(first, left, right)
            tiles[2 * h + 1, :, cols] = pltpu.roll(jnp.where(first, right, left), plane, 1)
        return 0

    lax.fori_loop(0, blk_count, tile, 0, unroll=4)

    def stand(d, _):
        found = mm_t(stretch[my_grp], masked[my_grp * blk_count + d])
        padded[1 : size_x + 1, pl.ds(d * size_y + 1, size_y)] = found.reshape(size_x, size_y, TALL, LANES)
        return 0

    lax.fori_loop(0, blk_count, stand, 0, unroll=4)

    near = 1 - my_grp
    lines = pl.ds(pl.multiple_of(jnp.where(my_grp == 0, 0, size_x - 1) * size_y * TALL, size_y * TALL), size_y * TALL)

    def stand_near(d, _):
        found = mm_t(stretch[near, lines, :], masked[near * blk_count + d])
        at_x = pl.ds(jnp.where(my_grp == 0, size_x + 1, 0), 1)
        padded[at_x, pl.ds(d * size_y + 1, size_y)] = found.reshape(1, size_y, TALL, LANES)
        return 0

    lax.fori_loop(0, blk_count, stand_near, 0, unroll=4)

    copy.wait()
    sub = iota((TALL, LANES), 0)

    def gather(group, _):
        found = [jnp.zeros((TALL, LANES), F32)] * 27
        for j in range(TALL):
            slot = slot_ref[0, group * TALL + j]
            d = slot // cap
            v = spots_s[d, my_blk * cap + slot % cap]
            x, y, z = v // (size_y * size_z), d * size_y + v // size_z % size_y, v % size_z
            for n in range(27):
                line = padded[x + 2 - n // 9, y + 2 - n // 3 % 3, pl.ds(z + 2 - n % 3, 1), :]
                found[n] = jnp.where(sub == j, jnp.broadcast_to(line, (TALL, LANES)), found[n])
        for n in range(27):
            gathered[n, pl.ds(pl.multiple_of(group * TALL, TALL), TALL), :] = found[n]
        return 0

    lax.fori_loop(0, rows // TALL, gather, 0)

    def backward(n, total):
        windows = jnp.concatenate([gathered[n * 3 + i] for i in range(3)], axis=1).astype(BF16)
        taps = jnp.concatenate([weight[n * 3 + i] for i in range(3)], axis=1)
        return total + mm_t(windows, taps)

    grad_rows[...] = lax.fori_loop(0, 9, backward, jnp.zeros((rows, channels), F32), unroll=9).astype(BF16)


def scene_kernel(
    dims,
    block0,
    block1,
    block2,
    block3,
    tiles,
    slot_rows,
    spots,
    padded,
    weight_grad,
    sent,
    slots,
    grid,
    shifted0,
    shifted1,
    acc_w,
    kept,
    sems,
):
    grp_count, blk_count, cap, rows, channels, size_x, size_y, size_z, scale = dims
    voxels = size_x * size_y * size_z
    devices = grp_count * blk_count
    plane = size_x * size_y
    blocks = (block0, block1, block2, block3)
    each = devices // 4
    my_grp, my_blk = lax.axis_index("grp"), lax.axis_index("blk")
    me = my_grp * blk_count + my_blk
    half = me % 2

    for k, block in enumerate(blocks):

        def fill(t, _, k=k, block=block):
            s = source(me, k, t, devices)
            chosen = rows_at(voxels, slot_rows[pl.ds(s, 1), :])
            held = mm(chosen, block[t]).astype(BF16)
            g, b = s // blk_count, s % blk_count
            place = pl.ds(pl.multiple_of(b * cap, cap), cap)
            for d in range(blk_count):
                slots[g * blk_count + d, place, :] = held[d * cap : (d + 1) * cap, :]
            return 0

        lax.fori_loop(0, each, fill, 0, unroll=4)

    def place_region(r, _):
        spot = spots[pl.ds(r, 1), :]
        key = spot % size_z * plane + spot // size_z
        found = mm(rows_at(voxels, key), slots[r]).astype(BF16)
        at = r % blk_count * LANES + r // blk_count * plane
        for z in range(size_z):
            grid[z, pl.ds(pl.multiple_of(at, plane), plane), :] = found[z * plane : (z + 1) * plane]
        return 0

    lax.fori_loop(0, devices, place_region, 0, unroll=4)

    def outer(dx, dy):
        g, d = my_grp + dx, my_blk + dy
        inside = (g >= 0) & (g < grp_count) & (d >= 0) & (d < blk_count)
        shape = ((1 if dx else size_x), (1 if dy else size_y), TALL, channels)
        at_x = {-1: 0, 0: 1, 1: size_x + 1}[dx]
        at_y = {-1: 0, 0: 1, 1: size_y + 1}[dy]
        there = (slice(at_x, at_x + shape[0]), slice(at_y, at_y + shape[1]))

        @pl.when(inside)
        def _():
            r = g * blk_count + d
            spot = spots[pl.ds(r, 1), :]
            key = spot // size_z * TALL + spot % size_z + 1
            t = iota((shape[0] * shape[1] * TALL, voxels), 0)
            x0, y0 = (size_x - 1 if dx < 0 else 0), (size_y - 1 if dy < 0 else 0)
            if dy and not dx:
                want = t // TALL * (size_y * TALL) + y0 * TALL + t % TALL
            else:
                want = t + (x0 * size_y + y0) * TALL
            padded[there] = mm(one_hot(want == key), slots[r]).reshape(shape)

        @pl.when(jnp.logical_not(inside))
        def _():
            padded[there] = jnp.zeros(shape, F32)

    for dx in (-1, 0, 1):
        for dy in (-1, 0, 1):
            outer(dx, dy)

    acc_w[...] = jnp.zeros(acc_w.shape, F32)
    offsets = ((-1, -1), (-1, 0), (-1, 1), (0, -1), (0, 0))
    sign = 1 - 2 * half
    lane = iota((LANES, LANES), 1)
    x, y = lane // size_y, lane % size_y
    nx = grp_count * size_x

    def mask(hits):
        return jnp.where(hits, 1.0, 0.0).astype(BF16)

    within, across = [], []
    for dx0, dy0 in offsets:
        dx, dy = sign * dx0, sign * dy0
        valid = (x - dx >= 0) & (x - dx < nx)
        stays = (y - dy >= 0) & (y - dy < size_y)
        within.append(mask(valid & stays))
        across.append(mask(valid & jnp.logical_not(stays)))

    def shift(z, d, there):
        def tile(dy):
            return tiles[z, :, pl.ds(pl.multiple_of((d + 1 - dy) * LANES, LANES), LANES)]

        own = tile(0)
        beside = {dy0: tile(sign * dy0) for dy0 in (-1, 1)}
        cols = pl.ds(pl.multiple_of(d * LANES, LANES), LANES)
        for m, (dx0, dy0) in enumerate(offsets):
            value = own
            if dx0 or dy0:
                ahead = sign * (dx0 * size_y + dy0)
                value = pltpu.roll(own, (ahead + LANES) % LANES, 1) * within[m]
            if dy0:
                ahead = sign * (dx0 * size_y + dy0 - dy0 * size_y)
                value = value + pltpu.roll(beside[dy0], (ahead + LANES) % LANES, 1) * across[m]
            there[m * LANES : (m + 1) * LANES, cols] = value

    def shift_first(d, _):
        shift(0, d, shifted0)
        return 0

    lax.fori_loop(0, blk_count, shift_first, 0, unroll=8)
    for z in range(size_z):
        here, there = (shifted0, shifted1) if z % 2 == 0 else (shifted1, shifted0)
        first, count = max(0, 1 - z), min(3, size_z + 1 - z) - max(0, 1 - z)
        share = -(-blk_count // count)

        def add(j, _, z=z, here=here, there=there, first=first, share=share):
            dz1 = first + j
            done = 0
            for m in range(5):
                rows_m = slice(m * LANES, (m + 1) * LANES)
                acc_w[dz1, rows_m] += mm(here[rows_m, :], grid[z + dz1 - 1])
                if z + 1 < size_z:
                    for i in range(done, share * (m + 1) // 5):
                        shift(z + 1, jnp.minimum(j * share + i, blk_count - 1), there)
                    done = share * (m + 1) // 5
            return 0

        lax.fori_loop(0, count, add, 0)

    def finish(dz1, _):
        done = (acc_w[dz1].T * scale).astype(BF16)
        for m in range(5):
            n = m + half * (4 - 2 * m)
            piece = done[:, m * LANES : (m + 1) * LANES]
            kept[n * 3 + dz1] = piece
        return 0

    lax.fori_loop(0, 3, finish, 0)
    mine = pltpu.make_async_copy(kept, weight_grad.at[pl.ds(12 * half, 15)], sems.at[0])
    theirs = pltpu.make_async_copy(kept.at[pl.ds(3 * half, 12)], sent, sems.at[1])
    theirs.start()
    mine.start()
    theirs.wait()
    mine.wait()


def place_kernel(received, mine, weight_grad, sem):
    other = 1 - lax.axis_index("blk") % 2
    copy = pltpu.make_async_copy(received, weight_grad.at[pl.ds(15 * other, 12)], sem)
    copy.start()
    copy.wait()


def output_kernel(sizes, padded, weight, spots, filled, output, acc_o):
    size_x, size_y, size_z = sizes
    voxels = size_x * size_y * size_z
    plane = size_x * size_y
    channels = weight.shape[1]
    me = lax.axis_index("grp") * lax.axis_size("blk") + lax.axis_index("blk")
    acc_o[...] = jnp.zeros(acc_o.shape, F32)

    def forward(n, _):
        dx, dy = n // 3, n % 3
        window = padded[pl.ds(dx, size_x), pl.ds(dy, size_y)].reshape(plane * TALL, channels)
        taps = jnp.concatenate([weight[n * 3 + i] for i in range(3)], axis=1)
        acc_o[...] += mm(window.astype(BF16), taps)
        return 0

    lax.fori_loop(0, 9, forward, 0, unroll=3)
    spot = spots[pl.ds(me, 1), :]
    key = jnp.where(filled[pl.ds(me, 1), :] > 0, spot // size_z * TALL + spot % size_z + 1, -1)
    occupied = mm(one_hot(iota((plane * TALL, voxels), 0) == key), jnp.ones((voxels, LANES), BF16))
    total = (
        pltpu.roll(acc_o[:, 0:LANES], 1, 0)
        + acc_o[:, LANES : 2 * LANES]
        + pltpu.roll(acc_o[:, 2 * LANES :], plane * TALL - 1, 0)
    )
    rounded = (total * occupied).astype(BF16)
    row, col = iota((voxels, plane * TALL), 0), iota((voxels, plane * TALL), 1)
    squeeze = one_hot(col == row // size_z * TALL + row % size_z + 1)
    output[...] = mm(squeeze, rounded).astype(BF16)


def exchange_masks(count):
    even = [1 << i for i in range(count.bit_length() - 2, 0, -1)]
    return even, even[1:] + even[:1]


def swap(value, count, masks):
    pairs = [(i, i ^ masks[i % 2]) for i in range(count)]
    return lax.ppermute(value, ("grp", "blk"), pairs)


def gather_all(block, count):
    even, odd = exchange_masks(count)
    held = block[None]
    for step in range(len(even) - 1):
        held = jnp.concatenate([held, swap(held, count, (even[step], odd[step]))], axis=0)
    last = swap(held, count, (even[-1], odd[-1]))
    return held, last, swap(held, count, (1, 1)), swap(last, count, (1, 1))


def gathered_shards(features, dest, placement, weight, grad_out):
    rows, channels = features.shape
    grp_count, blk_count = lax.axis_size("grp"), lax.axis_size("blk")
    devices = grp_count * blk_count
    size_x, size_y, size_z, out_channels = grad_out.shape
    sizes = (size_x, size_y, size_z)
    voxels = size_x * size_y * size_z
    plane = size_x * size_y
    cap = voxels // blk_count
    vmem = pl.BlockSpec(memory_space=pltpu.VMEM)
    smem = pl.BlockSpec(memory_space=pltpu.SMEM)
    hbm = pl.BlockSpec(memory_space=pl.ANY)
    packed, slot = pl.pallas_call(
        functools.partial(pack_kernel, sizes, cap),
        out_shape=(
            jax.ShapeDtypeStruct((voxels + 16, LANES), BF16),
            jax.ShapeDtypeStruct((1, rows), I32),
        ),
        in_specs=[vmem] * 3,
        out_specs=(vmem, vmem),
        name="pack",
    )(dest.reshape(1, rows), placement, grad_out.reshape(voxels, out_channels))
    cotangents = gather_all(packed, devices)
    cells = gather_all(features, devices)
    dims = (grp_count, blk_count, cap, rows, channels) + sizes
    grad_rows, tiles, slot_rows, spots, filled = pl.pallas_call(
        functools.partial(cotangent_kernel, dims),
        out_shape=(
            jax.ShapeDtypeStruct((rows, channels), BF16),
            jax.ShapeDtypeStruct((size_z, out_channels, (blk_count + 2) * LANES), BF16),
            jax.ShapeDtypeStruct((devices, rows), I32),
            jax.ShapeDtypeStruct((devices, voxels), I32),
            jax.ShapeDtypeStruct((devices, voxels), F32),
        ),
        in_specs=[smem] + [vmem] * 5,
        out_specs=(vmem,) * 5,
        scratch_shapes=[
            pltpu.VMEM((size_x + 2, blk_count * size_y + 2, TALL, out_channels), F32),
            pltpu.VMEM((27, rows, out_channels), F32),
            pltpu.VMEM((grp_count, plane * TALL, voxels), BF16),
            pltpu.VMEM((devices, LANES), F32),
            pltpu.VMEM((devices, voxels), F32),
            pltpu.VMEM((devices, out_channels, voxels), BF16),
            pltpu.SMEM((blk_count, voxels), I32),
            pltpu.SemaphoreType.DMA,
        ],
        compiler_params=pltpu.CompilerParams(vmem_limit_bytes=24 * 1024 * 1024),
        name="cotangent",
    )(slot, *cotangents, weight)
    scale = 1.0 / math.sqrt(rows * devices)
    padded, some, sent = pl.pallas_call(
        functools.partial(scene_kernel, dims + (scale,)),
        out_shape=(
            jax.ShapeDtypeStruct((size_x + 2, size_y + 2, TALL, channels), F32),
            jax.ShapeDtypeStruct(weight.shape, BF16),
            jax.ShapeDtypeStruct((12, channels, out_channels), BF16),
        ),
        in_specs=[vmem] * 7,
        out_specs=(vmem, hbm, hbm),
        scratch_shapes=[
            pltpu.VMEM((devices, voxels, channels), BF16),
            pltpu.VMEM((size_z, blk_count * LANES, channels), BF16),
            pltpu.VMEM((5 * out_channels, blk_count * LANES), BF16),
            pltpu.VMEM((5 * out_channels, blk_count * LANES), BF16),
            pltpu.VMEM((3, 5 * out_channels, channels), F32),
            pltpu.VMEM((15, channels, out_channels), BF16),
            pltpu.SemaphoreType.DMA((2,)),
        ],
        compiler_params=pltpu.CompilerParams(vmem_limit_bytes=24 * 1024 * 1024),
        name="scene",
    )(*cells, tiles, slot_rows, spots)
    received = swap(sent, devices, (1, 1))
    output = pl.pallas_call(
        functools.partial(output_kernel, sizes),
        out_shape=jax.ShapeDtypeStruct((voxels, out_channels), BF16),
        in_specs=[vmem] * 4,
        out_specs=vmem,
        scratch_shapes=[pltpu.VMEM((plane * TALL, 3 * out_channels), F32)],
        compiler_params=pltpu.CompilerParams(vmem_limit_bytes=8 * 1024 * 1024),
        name="output",
    )(padded, weight, spots, filled)
    weight_grad = pl.pallas_call(
        place_kernel,
        out_shape=jax.ShapeDtypeStruct(weight.shape, BF16),
        in_specs=[vmem, hbm],
        out_specs=hbm,
        scratch_shapes=[pltpu.SemaphoreType.DMA],
        input_output_aliases={1: 0},
        name="place",
    )(received, some)
    return output.reshape(grad_out.shape), grad_rows, weight_grad


def extended(cells, sides, width):
    for axis, dim in sides:
        count = lax.axis_size(axis)
        ends = count - 1
        head = lax.slice_in_dim(cells, 0, width, axis=dim)
        tail = lax.slice_in_dim(cells, cells.shape[dim] - width, cells.shape[dim], axis=dim)
        cells = jnp.concatenate(
            [
                lax.ppermute(tail, axis, [(i, (i + 1) % count) for i in range(ends)]),
                cells,
                lax.ppermute(head, axis, [((i + 1) % count, i) for i in range(ends)]),
            ],
            axis=dim,
        )
    return cells


def summed_shards(features, dest, placement, weight, grad_out):
    row_count, channels = features.shape
    blk_count = lax.axis_size("blk")
    grp_count = lax.axis_size("grp")
    voxel_of_slot = placement[0]
    voxel_count = voxel_of_slot.shape[0]
    capacity = voxel_count // blk_count
    size_x, size_y, size_z, out_channels = grad_out.shape
    target = dest[:, 0]
    owners = jnp.arange(blk_count, dtype=jnp.int32)
    one_hot = (target[:, None] == owners[None, :]).astype(jnp.int32)
    slot_rank = jnp.sum((jnp.cumsum(one_hot, axis=0) - one_hot) * one_hot, axis=1)
    send_counts = jnp.sum(one_hot, axis=0).reshape(blk_count, 1)
    slot_index = target * capacity + slot_rank
    outgoing = jnp.zeros((voxel_count, channels), jnp.bfloat16).at[slot_index].set(features)
    incoming, recv_counts = (
        lax.all_to_all(
            outgoing.reshape(blk_count, capacity, channels),
            "blk",
            split_axis=0,
            concat_axis=0,
            tiled=True,
        ),
        lax.all_to_all(send_counts, "blk", split_axis=0, concat_axis=0, tiled=True),
    )
    filled = (
        (jnp.arange(capacity, dtype=jnp.int32)[None, :] < recv_counts)
        .reshape(-1)
        .astype(jnp.float32)
    )
    voxel_rows = (
        jnp.zeros((voxel_count, channels), jnp.bfloat16)
        .at[voxel_of_slot]
        .set(incoming.reshape(voxel_count, channels))
    )
    occupied = jnp.zeros((voxel_count,), jnp.float32).at[voxel_of_slot].set(filled)[:, None]
    voxel_grid = voxel_rows.reshape(size_x, size_y, size_z, channels)
    padded = extended(voxel_grid, (("grp", 0), ("blk", 1)), 1)
    padded = jnp.pad(padded, ((0, 0), (0, 0), (1, 1), (0, 0)))
    shifted = []
    total = jnp.zeros((voxel_count, out_channels), jnp.float32)
    for offset in range(27):
        shift_x, shift_y, shift_z = (offset // 9, offset // 3 % 3, offset % 3)
        window = padded[
            shift_x : shift_x + size_x, shift_y : shift_y + size_y, shift_z : shift_z + size_z
        ].reshape(voxel_count, channels)
        shifted.append(window)
        total = total + jnp.dot(window, weight[offset], preferred_element_type=jnp.float32)
    output = (total * occupied).astype(jnp.bfloat16).reshape(size_x, size_y, size_z, out_channels)
    masked_grad = (
        grad_out.reshape(voxel_count, out_channels).astype(jnp.float32) * occupied
    ).astype(jnp.bfloat16)
    grad_padded = extended(
        masked_grad.reshape(size_x, size_y, size_z, out_channels), (("grp", 0), ("blk", 1)), 1
    )
    grad_padded = jnp.pad(grad_padded, ((0, 0), (0, 0), (1, 1), (0, 0)))
    back_total = jnp.zeros((voxel_count, channels), jnp.float32)
    partials = []
    for offset in range(27):
        shift_x, shift_y, shift_z = (offset // 9, offset // 3 % 3, offset % 3)
        window = grad_padded[
            2 - shift_x : 2 - shift_x + size_x,
            2 - shift_y : 2 - shift_y + size_y,
            2 - shift_z : 2 - shift_z + size_z,
        ].reshape(voxel_count, out_channels)
        back_total = back_total + lax.dot_general(
            window, weight[offset], (((1,), (1,)), ((), ())), preferred_element_type=jnp.float32
        )
        partials.append(
            lax.dot_general(
                shifted[offset],
                masked_grad,
                (((0,), (0,)), ((), ())),
                preferred_element_type=jnp.float32,
            )
        )
    grad_grid = (back_total * occupied).astype(jnp.bfloat16)
    weight_terms = jnp.stack(partials).reshape(27 * channels, out_channels)
    grad_scale = 1.0 / math.sqrt(row_count * blk_count * grp_count)
    weight_grad = (lax.psum(weight_terms, ("grp", "blk")) * grad_scale).astype(jnp.bfloat16)
    weight_grad = weight_grad.reshape(27, channels, out_channels)
    returning = grad_grid[voxel_of_slot].reshape(blk_count, capacity, channels)
    returned = lax.all_to_all(returning, "blk", split_axis=0, concat_axis=0, tiled=True)
    grad_rows = returned.reshape(voxel_count, channels)[slot_index]
    return (output, grad_rows, weight_grad)


def fits(mesh):
    grp_count, blk_count = mesh.shape["grp"], mesh.shape["blk"]
    return blk_count == 16 and grp_count == 2


def solution(mesh):
    in_specs = (
        P(("grp", "blk"), None),
        P(("grp", "blk"), None),
        P(("grp", "blk"), None),
        P(),
        P("grp", "blk", None, None),
    )
    out_specs = (P("grp", "blk", None, None), P(("grp", "blk"), None), P())
    shards = gathered_shards if fits(mesh) else summed_shards
    return jax.shard_map(shards, mesh=mesh, in_specs=in_specs, out_specs=out_specs, check_vma=False)
```

```python
import functools
import math

import jax
import jax.numpy as jnp
from jax import lax
from jax.experimental import pallas as pl
from jax.experimental.pallas import tpu as pltpu
from jax.sharding import PartitionSpec as P

LANES = 128
TALL = 8
F32, BF16, I32 = jnp.float32, jnp.bfloat16, jnp.int32


def iota(shape, axis):
    return lax.broadcasted_iota(I32, shape, axis)


def one_hot(hits):
    return jnp.where(hits, 1.0, 0.0).astype(BF16)


def rows_at(count, key):
    shape = (count, key.shape[1])
    places = iota(shape, 0).astype(BF16)
    return jnp.where(places == jnp.broadcast_to(key.astype(BF16), shape), 1.0, 0.0).astype(BF16)


def mm(a, b):
    return lax.dot_general(a, b, (((1,), (0,)), ((), ())), preferred_element_type=F32)


def mm_t(a, b):
    return lax.dot_general(a, b, (((1,), (1,)), ((), ())), preferred_element_type=F32)


def half_order(z, flat, group, plane):
    return z // 2 * (2 * plane) + (z + group) % 2 * plane + flat


def pack_kernel(sizes, cap, dest, placement, grad, packed, slots):
    size_x, size_y, size_z = sizes
    rows = dest.shape[1]
    voxels = grad.shape[0]
    plane = size_x * size_y
    lane = iota((rows, LANES), 1)
    upright = iota((rows, rows), 0) == iota((rows, rows), 1)
    target = jnp.sum(jnp.where(upright, dest[...], 0), axis=1, keepdims=True)
    named = one_hot(lane == target)
    earlier = one_hot(iota((rows, rows), 0) > iota((rows, rows), 1))
    rank = jnp.sum(mm(earlier, named) * named.astype(F32), axis=1, keepdims=True)
    slot = target.astype(F32) * cap + rank
    slot_row = jnp.sum(jnp.where(upright, slot, 0.0), axis=0, keepdims=True)
    counts = jnp.sum(named.astype(F32), axis=0, keepdims=True)
    slots[...] = slot_row.astype(I32)
    row, col = iota((voxels, voxels), 0), iota((voxels, voxels), 1)
    moved = half_order(row % size_z, row // size_z, lax.axis_index("grp"), plane)
    turned = mm(grad[...].astype(F32).T.astype(BF16), one_hot(col == moved)).astype(BF16)
    halves = voxels // LANES
    for h in range(halves):
        packed[h * LANES : (h + 1) * LANES, :] = turned[:, h * LANES : (h + 1) * LANES]
    spots = placement[...].astype(F32)
    index_rows = [slot_row, counts] + [spots[:, h * LANES : (h + 1) * LANES] for h in range(halves)]
    index_rows.append(jnp.zeros((16 - len(index_rows), LANES), F32))
    packed[halves * LANES : halves * LANES + 16, :] = jnp.concatenate(index_rows, axis=0).astype(BF16)


def source(me, buffer, t, count):
    even, odd = exchange_masks(count)

    def apart(masks):
        total = masks[-1] * (buffer % 2)
        for i in range(len(masks) - 1):
            total = total + (t >> i) % 2 * masks[i]
        return total

    holder = me ^ (buffer // 2)
    return holder ^ jnp.where(holder % 2 == 0, apart(even), apart(odd))


def cotangent_kernel(
    dims,
    slot_ref,
    block0,
    block1,
    block2,
    block3,
    weight,
    grad_rows,
    tiles,
    slot_rows,
    spots,
    filled,
    padded,
    gathered,
    stretch,
    counts,
    occupied,
    masked,
    spots_s,
    sem,
):
    grp_count, blk_count, cap, rows, channels, size_x, size_y, size_z = dims
    voxels = size_x * size_y * size_z
    devices = grp_count * blk_count
    plane = size_x * size_y
    halves = voxels // LANES
    blocks = (block0, block1, block2, block3)
    each = devices // 4
    my_grp, my_blk = lax.axis_index("grp"), lax.axis_index("blk")
    me = my_grp * blk_count + my_blk

    for k, block in enumerate(blocks):

        def read(t, _, k=k, block=block):
            s = source(me, k, t, devices)
            index = block[t, halves * LANES : halves * LANES + 16, :].astype(F32)
            slot_rows[pl.ds(s, 1), :] = index[0:1].astype(I32)
            counts[pl.ds(s, 1), :] = index[1:2]
            row = jnp.concatenate([index[2 + h : 3 + h] for h in range(halves)], axis=1)
            spots[pl.ds(s, 1), :] = row.astype(I32)
            return 0

        lax.fori_loop(0, each, read, 0, unroll=8)
    copy = pltpu.make_async_copy(
        spots.at[pl.ds(pl.multiple_of(my_grp * blk_count, blk_count), blk_count)], spots_s, sem
    )
    copy.start()

    spread = one_hot(iota((blk_count, voxels), 0) == iota((blk_count, voxels), 1) // cap)
    rank = (iota((blk_count, voxels), 1) % cap).astype(F32)
    for g in range(grp_count):
        sent = counts[g * blk_count : (g + 1) * blk_count, :].T[:blk_count].astype(BF16)
        held = jnp.where(rank < mm(sent, spread), 1.0, 0.0)
        filled[g * blk_count : (g + 1) * blk_count, :] = held
        row, col = iota((plane * TALL, voxels), 0), iota((plane * TALL, voxels), 1)
        z = row % TALL - 1
        inside = (z >= 0) & (z < size_z)
        stretch[g] = one_hot(inside & (col == half_order(z, row // TALL, g, plane)))

    zero_plane = jnp.zeros((1,) + padded.shape[1:], F32)
    zero_line = jnp.zeros((padded.shape[0], 1) + padded.shape[2:], F32)

    @pl.when(my_grp == 0)
    def _():
        padded[0:1] = zero_plane

    @pl.when(my_grp == grp_count - 1)
    def _():
        padded[size_x + 1 : size_x + 2] = zero_plane

    padded[:, 0:1] = zero_line
    padded[:, padded.shape[1] - 1 :] = zero_line
    for z in range(size_z):
        tiles[z, :, 0:LANES] = jnp.zeros((LANES, LANES), BF16)
        tiles[z, :, (blk_count + 1) * LANES :] = jnp.zeros((LANES, LANES), BF16)

    def occupy(r, _):
        spot = spots[pl.ds(r, 1), :]
        key = half_order(spot % size_z, spot // size_z, r // blk_count, plane)
        held = jnp.broadcast_to(filled[pl.ds(r, 1), :], (16, voxels)).astype(BF16)
        occupied[pl.ds(r, 1), :] = mm_t(held, rows_at(voxels, key))[0:1]
        return 0

    lax.fori_loop(0, devices, occupy, 0, unroll=16)

    for k, block in enumerate(blocks):

        def mask(t, _, k=k, block=block):
            r = source(me, k, t, devices)
            there = occupied[pl.ds(r, 1), :].astype(BF16)
            for h in range(halves):
                at = slice(h * LANES, (h + 1) * LANES)
                masked[r, :, at] = block[t, at, :] * there[:, at]
            return 0

        lax.fori_loop(0, each, mask, 0, unroll=8)

    first = iota((LANES, LANES), 1) < plane

    def tile(d, _):
        cols = pl.ds(pl.multiple_of((d + 1) * LANES, LANES), LANES)
        for h in range(halves):
            at = slice(h * LANES, (h + 1) * LANES)
            left, right = masked[d, :, at], masked[blk_count + d, :, at]
            tiles[2 * h, :, cols] = jnp.where(first, left, right)
            tiles[2 * h + 1, :, cols] = pltpu.roll(jnp.where(first, right, left), plane, 1)
        return 0

    lax.fori_loop(0, blk_count, tile, 0, unroll=8)

    def stand(d, _):
        found = mm_t(stretch[my_grp], masked[my_grp * blk_count + d])
        padded[1 : size_x + 1, pl.ds(d * size_y + 1, size_y)] = found.reshape(size_x, size_y, TALL, LANES)
        return 0

    lax.fori_loop(0, blk_count, stand, 0, unroll=8)

    near = 1 - my_grp
    lines = pl.ds(pl.multiple_of(jnp.where(my_grp == 0, 0, size_x - 1) * size_y * TALL, size_y * TALL), size_y * TALL)

    def stand_near(d, _):
        found = mm_t(stretch[near, lines, :], masked[near * blk_count + d])
        at_x = pl.ds(jnp.where(my_grp == 0, size_x + 1, 0), 1)
        padded[at_x, pl.ds(d * size_y + 1, size_y)] = found.reshape(1, size_y, TALL, LANES)
        return 0

    lax.fori_loop(0, blk_count, stand_near, 0, unroll=16)

    copy.wait()
    sub = iota((TALL, LANES), 0)

    def gather(group, _):
        found = [jnp.zeros((TALL, LANES), F32)] * 27
        for j in range(TALL):
            slot = slot_ref[0, group * TALL + j]
            d = slot // cap
            v = spots_s[d, my_blk * cap + slot % cap]
            x, y, z = v // (size_y * size_z), d * size_y + v // size_z % size_y, v % size_z
            for n in range(27):
                line = padded[x + 2 - n // 9, y + 2 - n // 3 % 3, pl.ds(z + 2 - n % 3, 1), :]
                found[n] = jnp.where(sub == j, jnp.broadcast_to(line, (TALL, LANES)), found[n])
        for n in range(27):
            gathered[n, pl.ds(pl.multiple_of(group * TALL, TALL), TALL), :] = found[n]
        return 0

    lax.fori_loop(0, rows // TALL, gather, 0)

    def backward(n, total):
        windows = jnp.concatenate([gathered[n * 3 + i] for i in range(3)], axis=1).astype(BF16)
        taps = jnp.concatenate([weight[n * 3 + i] for i in range(3)], axis=1)
        return total + mm_t(windows, taps)

    grad_rows[...] = lax.fori_loop(0, 9, backward, jnp.zeros((rows, channels), F32), unroll=9).astype(BF16)


def scene_kernel(
    dims,
    block0,
    block1,
    block2,
    block3,
    tiles,
    slot_rows,
    spots,
    padded,
    weight_grad,
    sent,
    slots,
    grid,
    shifted0,
    shifted1,
    acc_w,
    sem,
):
    grp_count, blk_count, cap, rows, channels, size_x, size_y, size_z, scale = dims
    voxels = size_x * size_y * size_z
    devices = grp_count * blk_count
    plane = size_x * size_y
    blocks = (block0, block1, block2, block3)
    each = devices // 4
    my_grp, my_blk = lax.axis_index("grp"), lax.axis_index("blk")
    me = my_grp * blk_count + my_blk
    half = me % 2

    for k, block in enumerate(blocks):

        def fill(t, _, k=k, block=block):
            s = source(me, k, t, devices)
            chosen = rows_at(voxels, slot_rows[pl.ds(s, 1), :])
            held = mm(chosen, block[t]).astype(BF16)
            g, b = s // blk_count, s % blk_count
            place = pl.ds(pl.multiple_of(b * cap, cap), cap)
            for d in range(blk_count):
                slots[g * blk_count + d, place, :] = held[d * cap : (d + 1) * cap, :]
            return 0

        lax.fori_loop(0, each, fill, 0, unroll=8)

    def place_region(r, _):
        spot = spots[pl.ds(r, 1), :]
        key = spot % size_z * plane + spot // size_z
        found = mm(rows_at(voxels, key), slots[r]).astype(BF16)
        at = r % blk_count * LANES + r // blk_count * plane
        for z in range(size_z):
            grid[z, pl.ds(pl.multiple_of(at, plane), plane), :] = found[z * plane : (z + 1) * plane]
        return 0

    lax.fori_loop(0, devices, place_region, 0, unroll=8)

    def outer(dx, dy):
        g, d = my_grp + dx, my_blk + dy
        inside = (g >= 0) & (g < grp_count) & (d >= 0) & (d < blk_count)
        shape = ((1 if dx else size_x), (1 if dy else size_y), TALL, channels)
        at_x = {-1: 0, 0: 1, 1: size_x + 1}[dx]
        at_y = {-1: 0, 0: 1, 1: size_y + 1}[dy]
        there = (slice(at_x, at_x + shape[0]), slice(at_y, at_y + shape[1]))

        @pl.when(inside)
        def _():
            r = g * blk_count + d
            spot = spots[pl.ds(r, 1), :]
            key = spot // size_z * TALL + spot % size_z + 1
            t = iota((shape[0] * shape[1] * TALL, voxels), 0)
            x0, y0 = (size_x - 1 if dx < 0 else 0), (size_y - 1 if dy < 0 else 0)
            if dy and not dx:
                want = t // TALL * (size_y * TALL) + y0 * TALL + t % TALL
            else:
                want = t + (x0 * size_y + y0) * TALL
            padded[there] = mm(one_hot(want == key), slots[r]).reshape(shape)

        @pl.when(jnp.logical_not(inside))
        def _():
            padded[there] = jnp.zeros(shape, F32)

    for dx in (-1, 0, 1):
        for dy in (-1, 0, 1):
            outer(dx, dy)

    acc_w[...] = jnp.zeros(acc_w.shape, F32)
    offsets = ((-1, -1), (-1, 0), (-1, 1), (0, -1), (0, 0))
    sign = 1 - 2 * half
    lane = iota((LANES, LANES), 1)
    x, y = lane // size_y, lane % size_y
    nx = grp_count * size_x

    def mask(hits):
        return jnp.where(hits, 1.0, 0.0).astype(BF16)

    within, across = [], []
    for dx0, dy0 in offsets:
        dx, dy = sign * dx0, sign * dy0
        valid = (x - dx >= 0) & (x - dx < nx)
        stays = (y - dy >= 0) & (y - dy < size_y)
        within.append(mask(valid & stays))
        across.append(mask(valid & jnp.logical_not(stays)))

    def shift(z, d, there):
        def tile(dy):
            return tiles[z, :, pl.ds(pl.multiple_of((d + 1 - dy) * LANES, LANES), LANES)]

        own = tile(0)
        beside = {dy0: tile(sign * dy0) for dy0 in (-1, 1)}
        cols = pl.ds(pl.multiple_of(d * LANES, LANES), LANES)
        for m, (dx0, dy0) in enumerate(offsets):
            value = own
            if dx0 or dy0:
                ahead = sign * (dx0 * size_y + dy0)
                value = pltpu.roll(own, (ahead + LANES) % LANES, 1) * within[m]
            if dy0:
                ahead = sign * (dx0 * size_y + dy0 - dy0 * size_y)
                value = value + pltpu.roll(beside[dy0], (ahead + LANES) % LANES, 1) * across[m]
            there[m * LANES : (m + 1) * LANES, cols] = value

    def shift_first(d, _):
        shift(0, d, shifted0)
        return 0

    lax.fori_loop(0, blk_count, shift_first, 0, unroll=16)
    for z in range(size_z):
        here, there = (shifted0, shifted1) if z % 2 == 0 else (shifted1, shifted0)
        first, count = max(0, 1 - z), min(3, size_z + 1 - z) - max(0, 1 - z)
        share = -(-blk_count // count)

        def add(j, _, z=z, here=here, there=there, first=first, share=share):
            dz1 = first + j
            done = 0
            for m in range(5):
                rows_m = slice(m * LANES, (m + 1) * LANES)
                acc_w[dz1, rows_m] += mm(here[rows_m, :], grid[z + dz1 - 1])
                if z + 1 < size_z:
                    for i in range(done, share * (m + 1) // 5):
                        shift(z + 1, jnp.minimum(j * share + i, blk_count - 1), there)
                    done = share * (m + 1) // 5
            return 0

        lax.fori_loop(0, count, add, 0)

    def finish(dz1, _):
        done = (acc_w[dz1].T * scale).astype(BF16)
        for m in range(5):
            n = m + half * (4 - 2 * m)
            piece = done[:, m * LANES : (m + 1) * LANES]
            weight_grad[n * 3 + dz1] = piece
        return 0

    lax.fori_loop(0, 3, finish, 0, unroll=3)
    theirs = pltpu.make_async_copy(weight_grad.at[pl.ds(3 * half, 12)], sent, sem)
    theirs.start()
    theirs.wait()


def output_kernel(sizes, padded, weight, spots, filled, mine, received, output, weight_grad, acc_o, sems):
    half = lax.axis_index("blk") % 2
    copies = (
        pltpu.make_async_copy(mine, weight_grad.at[pl.ds(12 * half, 15)], sems.at[0]),
        pltpu.make_async_copy(received, weight_grad.at[pl.ds(15 * (1 - half), 12)], sems.at[1]),
    )
    for copy in copies:
        copy.start()
    size_x, size_y, size_z = sizes
    voxels = size_x * size_y * size_z
    plane = size_x * size_y
    channels = weight.shape[1]
    me = lax.axis_index("grp") * lax.axis_size("blk") + lax.axis_index("blk")
    acc_o[...] = jnp.zeros(acc_o.shape, F32)

    def forward(n, _):
        dx, dy = n // 3, n % 3
        window = padded[pl.ds(dx, size_x), pl.ds(dy, size_y)].reshape(plane * TALL, channels)
        taps = jnp.concatenate([weight[n * 3 + i] for i in range(3)], axis=1)
        acc_o[...] += mm(window.astype(BF16), taps)
        return 0

    lax.fori_loop(0, 9, forward, 0, unroll=9)
    spot = spots[pl.ds(me, 1), :]
    key = jnp.where(filled[pl.ds(me, 1), :] > 0, spot // size_z * TALL + spot % size_z + 1, -1)
    occupied = mm(one_hot(iota((plane * TALL, voxels), 0) == key), jnp.ones((voxels, LANES), BF16))
    total = (
        pltpu.roll(acc_o[:, 0:LANES], 1, 0)
        + acc_o[:, LANES : 2 * LANES]
        + pltpu.roll(acc_o[:, 2 * LANES :], plane * TALL - 1, 0)
    )
    rounded = (total * occupied).astype(BF16)
    row, col = iota((voxels, plane * TALL), 0), iota((voxels, plane * TALL), 1)
    squeeze = one_hot(col == row // size_z * TALL + row % size_z + 1)
    output[...] = mm(squeeze, rounded).astype(BF16)
    for copy in copies:
        copy.wait()


def exchange_masks(count):
    even = [1 << i for i in range(count.bit_length() - 2, 0, -1)]
    return even, even[1:] + even[:1]


def swap(value, count, masks):
    pairs = [(i, i ^ masks[i % 2]) for i in range(count)]
    return lax.ppermute(value, ("grp", "blk"), pairs)


def after(value, *others):
    return lax.optimization_barrier((value,) + others)[0]


def gather_all(block, count):
    even, odd = exchange_masks(count)
    held = block[None]
    for step in range(len(even) - 1):
        held = jnp.concatenate([held, swap(held, count, (even[step], odd[step]))], axis=0)
        if step == 0 and block.shape[1] == LANES:
            held = after(held)
    last = swap(held, count, (even[-1], odd[-1]))
    return held, last, swap(held, count, (1, 1)), swap(last, count, (1, 1))


def gathered_shards(features, dest, placement, weight, grad_out):
    rows, channels = features.shape
    grp_count, blk_count = lax.axis_size("grp"), lax.axis_size("blk")
    devices = grp_count * blk_count
    size_x, size_y, size_z, out_channels = grad_out.shape
    sizes = (size_x, size_y, size_z)
    voxels = size_x * size_y * size_z
    plane = size_x * size_y
    cap = voxels // blk_count
    vmem = pl.BlockSpec(memory_space=pltpu.VMEM)
    smem = pl.BlockSpec(memory_space=pltpu.SMEM)
    hbm = pl.BlockSpec(memory_space=pl.ANY)
    packed, slot = pl.pallas_call(
        functools.partial(pack_kernel, sizes, cap),
        out_shape=(
            jax.ShapeDtypeStruct((voxels + 16, LANES), BF16),
            jax.ShapeDtypeStruct((1, rows), I32),
        ),
        in_specs=[vmem] * 3,
        out_specs=(vmem, vmem),
        name="pack",
    )(dest.reshape(1, rows), placement, grad_out.reshape(voxels, out_channels))
    cotangents = gather_all(packed, devices)
    cells = gather_all(features, devices)
    dims = (grp_count, blk_count, cap, rows, channels) + sizes
    grad_rows, tiles, slot_rows, spots, filled = pl.pallas_call(
        functools.partial(cotangent_kernel, dims),
        out_shape=(
            jax.ShapeDtypeStruct((rows, channels), BF16),
            jax.ShapeDtypeStruct((size_z, out_channels, (blk_count + 2) * LANES), BF16),
            jax.ShapeDtypeStruct((devices, rows), I32),
            jax.ShapeDtypeStruct((devices, voxels), I32),
            jax.ShapeDtypeStruct((devices, voxels), F32),
        ),
        in_specs=[smem] + [vmem] * 5,
        out_specs=(vmem,) * 5,
        scratch_shapes=[
            pltpu.VMEM((size_x + 2, blk_count * size_y + 2, TALL, out_channels), F32),
            pltpu.VMEM((27, rows, out_channels), F32),
            pltpu.VMEM((grp_count, plane * TALL, voxels), BF16),
            pltpu.VMEM((devices, LANES), F32),
            pltpu.VMEM((devices, voxels), F32),
            pltpu.VMEM((devices, out_channels, voxels), BF16),
            pltpu.SMEM((blk_count, voxels), I32),
            pltpu.SemaphoreType.DMA,
        ],
        compiler_params=pltpu.CompilerParams(vmem_limit_bytes=24 * 1024 * 1024),
        name="cotangent",
    )(slot, *cotangents, weight)
    scale = 1.0 / math.sqrt(rows * devices)
    padded, some, sent = pl.pallas_call(
        functools.partial(scene_kernel, dims + (scale,)),
        out_shape=(
            jax.ShapeDtypeStruct((size_x + 2, size_y + 2, TALL, channels), F32),
            jax.ShapeDtypeStruct((15, channels, out_channels), BF16),
            jax.ShapeDtypeStruct((12, channels, out_channels), BF16),
        ),
        in_specs=[vmem] * 7,
        out_specs=(vmem, vmem, hbm),
        scratch_shapes=[
            pltpu.VMEM((devices, voxels, channels), BF16),
            pltpu.VMEM((size_z, blk_count * LANES, channels), BF16),
            pltpu.VMEM((5 * out_channels, blk_count * LANES), BF16),
            pltpu.VMEM((5 * out_channels, blk_count * LANES), BF16),
            pltpu.VMEM((3, 5 * out_channels, channels), F32),
            pltpu.SemaphoreType.DMA,
        ],
        compiler_params=pltpu.CompilerParams(vmem_limit_bytes=24 * 1024 * 1024),
        name="scene",
    )(*cells, tiles, slot_rows, spots)
    received = swap(sent, devices, (1, 1))
    output, weight_grad = pl.pallas_call(
        functools.partial(output_kernel, sizes),
        out_shape=(
            jax.ShapeDtypeStruct((voxels, out_channels), BF16),
            jax.ShapeDtypeStruct(weight.shape, BF16),
        ),
        in_specs=[vmem] * 6,
        out_specs=(vmem, hbm),
        scratch_shapes=[
            pltpu.VMEM((plane * TALL, 3 * out_channels), F32),
            pltpu.SemaphoreType.DMA((2,)),
        ],
        compiler_params=pltpu.CompilerParams(vmem_limit_bytes=12 * 1024 * 1024),
        name="output",
    )(padded, weight, spots, filled, some, received)
    return output.reshape(grad_out.shape), grad_rows, weight_grad


def extended(cells, sides, width):
    for axis, dim in sides:
        count = lax.axis_size(axis)
        ends = count - 1
        head = lax.slice_in_dim(cells, 0, width, axis=dim)
        tail = lax.slice_in_dim(cells, cells.shape[dim] - width, cells.shape[dim], axis=dim)
        cells = jnp.concatenate(
            [
                lax.ppermute(tail, axis, [(i, (i + 1) % count) for i in range(ends)]),
                cells,
                lax.ppermute(head, axis, [((i + 1) % count, i) for i in range(ends)]),
            ],
            axis=dim,
        )
    return cells


def summed_shards(features, dest, placement, weight, grad_out):
    row_count, channels = features.shape
    blk_count = lax.axis_size("blk")
    grp_count = lax.axis_size("grp")
    voxel_of_slot = placement[0]
    voxel_count = voxel_of_slot.shape[0]
    capacity = voxel_count // blk_count
    size_x, size_y, size_z, out_channels = grad_out.shape
    target = dest[:, 0]
    owners = jnp.arange(blk_count, dtype=jnp.int32)
    one_hot = (target[:, None] == owners[None, :]).astype(jnp.int32)
    slot_rank = jnp.sum((jnp.cumsum(one_hot, axis=0) - one_hot) * one_hot, axis=1)
    send_counts = jnp.sum(one_hot, axis=0).reshape(blk_count, 1)
    slot_index = target * capacity + slot_rank
    outgoing = jnp.zeros((voxel_count, channels), jnp.bfloat16).at[slot_index].set(features)
    incoming, recv_counts = (
        lax.all_to_all(
            outgoing.reshape(blk_count, capacity, channels),
            "blk",
            split_axis=0,
            concat_axis=0,
            tiled=True,
        ),
        lax.all_to_all(send_counts, "blk", split_axis=0, concat_axis=0, tiled=True),
    )
    filled = (
        (jnp.arange(capacity, dtype=jnp.int32)[None, :] < recv_counts)
        .reshape(-1)
        .astype(jnp.float32)
    )
    voxel_rows = (
        jnp.zeros((voxel_count, channels), jnp.bfloat16)
        .at[voxel_of_slot]
        .set(incoming.reshape(voxel_count, channels))
    )
    occupied = jnp.zeros((voxel_count,), jnp.float32).at[voxel_of_slot].set(filled)[:, None]
    voxel_grid = voxel_rows.reshape(size_x, size_y, size_z, channels)
    padded = extended(voxel_grid, (("grp", 0), ("blk", 1)), 1)
    padded = jnp.pad(padded, ((0, 0), (0, 0), (1, 1), (0, 0)))
    shifted = []
    total = jnp.zeros((voxel_count, out_channels), jnp.float32)
    for offset in range(27):
        shift_x, shift_y, shift_z = (offset // 9, offset // 3 % 3, offset % 3)
        window = padded[
            shift_x : shift_x + size_x, shift_y : shift_y + size_y, shift_z : shift_z + size_z
        ].reshape(voxel_count, channels)
        shifted.append(window)
        total = total + jnp.dot(window, weight[offset], preferred_element_type=jnp.float32)
    output = (total * occupied).astype(jnp.bfloat16).reshape(size_x, size_y, size_z, out_channels)
    masked_grad = (
        grad_out.reshape(voxel_count, out_channels).astype(jnp.float32) * occupied
    ).astype(jnp.bfloat16)
    grad_padded = extended(
        masked_grad.reshape(size_x, size_y, size_z, out_channels), (("grp", 0), ("blk", 1)), 1
    )
    grad_padded = jnp.pad(grad_padded, ((0, 0), (0, 0), (1, 1), (0, 0)))
    back_total = jnp.zeros((voxel_count, channels), jnp.float32)
    partials = []
    for offset in range(27):
        shift_x, shift_y, shift_z = (offset // 9, offset // 3 % 3, offset % 3)
        window = grad_padded[
            2 - shift_x : 2 - shift_x + size_x,
            2 - shift_y : 2 - shift_y + size_y,
            2 - shift_z : 2 - shift_z + size_z,
        ].reshape(voxel_count, out_channels)
        back_total = back_total + lax.dot_general(
            window, weight[offset], (((1,), (1,)), ((), ())), preferred_element_type=jnp.float32
        )
        partials.append(
            lax.dot_general(
                shifted[offset],
                masked_grad,
                (((0,), (0,)), ((), ())),
                preferred_element_type=jnp.float32,
            )
        )
    grad_grid = (back_total * occupied).astype(jnp.bfloat16)
    weight_terms = jnp.stack(partials).reshape(27 * channels, out_channels)
    grad_scale = 1.0 / math.sqrt(row_count * blk_count * grp_count)
    weight_grad = (lax.psum(weight_terms, ("grp", "blk")) * grad_scale).astype(jnp.bfloat16)
    weight_grad = weight_grad.reshape(27, channels, out_channels)
    returning = grad_grid[voxel_of_slot].reshape(blk_count, capacity, channels)
    returned = lax.all_to_all(returning, "blk", split_axis=0, concat_axis=0, tiled=True)
    grad_rows = returned.reshape(voxel_count, channels)[slot_index]
    return (output, grad_rows, weight_grad)


def fits(mesh):
    grp_count, blk_count = mesh.shape["grp"], mesh.shape["blk"]
    return blk_count == 16 and grp_count == 2


def solution(mesh):
    in_specs = (
        P(("grp", "blk"), None),
        P(("grp", "blk"), None),
        P(("grp", "blk"), None),
        P(),
        P("grp", "blk", None, None),
    )
    out_specs = (P("grp", "blk", None, None), P(("grp", "blk"), None), P())
    shards = gathered_shards if fits(mesh) else summed_shards
    return jax.shard_map(shards, mesh=mesh, in_specs=in_specs, out_specs=out_specs, check_vma=False)
```

```python
import functools
import math

import jax
import jax.numpy as jnp
from jax import lax
from jax.experimental import pallas as pl
from jax.experimental.pallas import tpu as pltpu
from jax.sharding import PartitionSpec as P

LANES = 128
TALL = 8
F32, BF16, I32 = jnp.float32, jnp.bfloat16, jnp.int32


def iota(shape, axis):
    return lax.broadcasted_iota(I32, shape, axis)


def one_hot(hits):
    return jnp.where(hits, 1.0, 0.0).astype(BF16)


def rows_at(count, key):
    shape = (count, key.shape[1])
    places = iota(shape, 0).astype(BF16)
    return jnp.where(places == jnp.broadcast_to(key.astype(BF16), shape), 1.0, 0.0).astype(BF16)


def mm(a, b):
    return lax.dot_general(a, b, (((1,), (0,)), ((), ())), preferred_element_type=F32)


def mm_t(a, b):
    return lax.dot_general(a, b, (((1,), (1,)), ((), ())), preferred_element_type=F32)


def half_order(z, flat, group, plane):
    return z // 2 * (2 * plane) + (z + group) % 2 * plane + flat


def pack_kernel(sizes, cap, dest, placement, grad, packed, slots):
    size_x, size_y, size_z = sizes
    rows = dest.shape[1]
    voxels = grad.shape[0]
    plane = size_x * size_y
    lane = iota((rows, LANES), 1)
    upright = iota((rows, rows), 0) == iota((rows, rows), 1)
    target = jnp.sum(jnp.where(upright, dest[...], 0), axis=1, keepdims=True)
    named = one_hot(lane == target)
    earlier = one_hot(iota((rows, rows), 0) > iota((rows, rows), 1))
    rank = jnp.sum(mm(earlier, named) * named.astype(F32), axis=1, keepdims=True)
    slot = target.astype(F32) * cap + rank
    slot_row = jnp.sum(jnp.where(upright, slot, 0.0), axis=0, keepdims=True)
    counts = jnp.sum(named.astype(F32), axis=0, keepdims=True)
    slots[...] = slot_row.astype(I32)
    row, col = iota((voxels, voxels), 0), iota((voxels, voxels), 1)
    moved = half_order(row % size_z, row // size_z, lax.axis_index("grp"), plane)
    turned = mm(grad[...].astype(F32).T.astype(BF16), one_hot(col == moved)).astype(BF16)
    halves = voxels // LANES
    for h in range(halves):
        packed[h * LANES : (h + 1) * LANES, :] = turned[:, h * LANES : (h + 1) * LANES]
    spots = placement[...].astype(F32)
    index_rows = [slot_row, counts] + [spots[:, h * LANES : (h + 1) * LANES] for h in range(halves)]
    index_rows.append(jnp.zeros((16 - len(index_rows), LANES), F32))
    packed[halves * LANES : halves * LANES + 16, :] = jnp.concatenate(index_rows, axis=0).astype(BF16)


def source(me, buffer, t, count):
    even, odd = exchange_masks(count)

    def apart(masks):
        total = masks[-1] * (buffer % 2)
        for i in range(len(masks) - 1):
            total = total + (t >> i) % 2 * masks[i]
        return total

    holder = me ^ (buffer // 2)
    return holder ^ jnp.where(holder % 2 == 0, apart(even), apart(odd))


def cotangent_kernel(
    dims,
    slot_ref,
    block0,
    block1,
    block2,
    block3,
    weight,
    grad_rows,
    tiles,
    slot_rows,
    spots,
    filled,
    padded,
    gathered,
    stretch,
    counts,
    occupied,
    masked,
    fetched,
    spots_s,
    sem,
    fetch_sems,
):
    grp_count, blk_count, cap, rows, channels, size_x, size_y, size_z = dims
    voxels = size_x * size_y * size_z
    devices = grp_count * blk_count
    plane = size_x * size_y
    halves = voxels // LANES
    far = (block1, block2, block3)
    fetches = [pltpu.make_async_copy(far[k], fetched.at[k], fetch_sems.at[k]) for k in range(3)]
    for fetch in fetches:
        fetch.start()
    blocks = (block0, fetched.at[0], fetched.at[1], fetched.at[2])
    each = devices // 4
    my_grp, my_blk = lax.axis_index("grp"), lax.axis_index("blk")
    me = my_grp * blk_count + my_blk

    for g in range(grp_count):
        row, col = iota((plane * TALL, voxels), 0), iota((plane * TALL, voxels), 1)
        z = row % TALL - 1
        inside = (z >= 0) & (z < size_z)
        stretch[g] = one_hot(inside & (col == half_order(z, row // TALL, g, plane)))

    zero_plane = jnp.zeros((1,) + padded.shape[1:], F32)
    zero_line = jnp.zeros((padded.shape[0], 1) + padded.shape[2:], F32)

    @pl.when(my_grp == 0)
    def _():
        padded[0:1] = zero_plane

    @pl.when(my_grp == grp_count - 1)
    def _():
        padded[size_x + 1 : size_x + 2] = zero_plane

    padded[:, 0:1] = zero_line
    padded[:, padded.shape[1] - 1 :] = zero_line
    for z in range(size_z):
        tiles[z, :, 0:LANES] = jnp.zeros((LANES, LANES), BF16)
        tiles[z, :, (blk_count + 1) * LANES :] = jnp.zeros((LANES, LANES), BF16)

    for k, block in enumerate(blocks):

        def read(t, _, k=k, block=block):
            s = source(me, k, t, devices)
            index = block[t, halves * LANES : halves * LANES + 16, :].astype(F32)
            slot_rows[pl.ds(s, 1), :] = index[0:1].astype(I32)
            counts[pl.ds(s, 1), :] = index[1:2]
            row = jnp.concatenate([index[2 + h : 3 + h] for h in range(halves)], axis=1)
            spots[pl.ds(s, 1), :] = row.astype(I32)
            return 0

        if k:
            fetches[k - 1].wait()
        lax.fori_loop(0, each, read, 0, unroll=8)
    copy = pltpu.make_async_copy(
        spots.at[pl.ds(pl.multiple_of(my_grp * blk_count, blk_count), blk_count)], spots_s, sem
    )
    copy.start()

    spread = one_hot(iota((blk_count, voxels), 0) == iota((blk_count, voxels), 1) // cap)
    rank = (iota((blk_count, voxels), 1) % cap).astype(F32)
    for g in range(grp_count):
        sent = counts[g * blk_count : (g + 1) * blk_count, :].T[:blk_count].astype(BF16)
        held = jnp.where(rank < mm(sent, spread), 1.0, 0.0)
        filled[g * blk_count : (g + 1) * blk_count, :] = held

    def occupy(r, _):
        spot = spots[pl.ds(r, 1), :]
        key = half_order(spot % size_z, spot // size_z, r // blk_count, plane)
        held = jnp.broadcast_to(filled[pl.ds(r, 1), :], (16, voxels)).astype(BF16)
        occupied[pl.ds(r, 1), :] = mm_t(held, rows_at(voxels, key))[0:1]
        return 0

    lax.fori_loop(0, devices, occupy, 0, unroll=32)

    for k, block in enumerate(blocks):

        def mask(t, _, k=k, block=block):
            r = source(me, k, t, devices)
            there = occupied[pl.ds(r, 1), :].astype(BF16)
            for h in range(halves):
                at = slice(h * LANES, (h + 1) * LANES)
                masked[r, :, at] = block[t, at, :] * there[:, at]
            return 0

        lax.fori_loop(0, each, mask, 0, unroll=8)

    first = iota((LANES, LANES), 1) < plane

    def tile(d, _):
        cols = pl.ds(pl.multiple_of((d + 1) * LANES, LANES), LANES)
        for h in range(halves):
            at = slice(h * LANES, (h + 1) * LANES)
            left, right = masked[d, :, at], masked[blk_count + d, :, at]
            tiles[2 * h, :, cols] = jnp.where(first, left, right)
            tiles[2 * h + 1, :, cols] = pltpu.roll(jnp.where(first, right, left), plane, 1)
        return 0

    lax.fori_loop(0, blk_count, tile, 0, unroll=8)

    def stand(d, _):
        found = mm_t(stretch[my_grp], masked[my_grp * blk_count + d])
        padded[1 : size_x + 1, pl.ds(d * size_y + 1, size_y)] = found.reshape(size_x, size_y, TALL, LANES)
        return 0

    lax.fori_loop(0, blk_count, stand, 0, unroll=8)

    near = 1 - my_grp
    lines = pl.ds(pl.multiple_of(jnp.where(my_grp == 0, 0, size_x - 1) * size_y * TALL, size_y * TALL), size_y * TALL)

    def stand_near(d, _):
        found = mm_t(stretch[near, lines, :], masked[near * blk_count + d])
        at_x = pl.ds(jnp.where(my_grp == 0, size_x + 1, 0), 1)
        padded[at_x, pl.ds(d * size_y + 1, size_y)] = found.reshape(1, size_y, TALL, LANES)
        return 0

    lax.fori_loop(0, blk_count, stand_near, 0, unroll=16)

    copy.wait()
    sub = iota((TALL, LANES), 0)

    def gather(group, _):
        found = [jnp.zeros((TALL, LANES), F32)] * 27
        for j in range(TALL):
            slot = slot_ref[0, group * TALL + j]
            d = slot // cap
            v = spots_s[d, my_blk * cap + slot % cap]
            x, y, z = v // (size_y * size_z), d * size_y + v // size_z % size_y, v % size_z
            for n in range(27):
                line = padded[x + 2 - n // 9, y + 2 - n // 3 % 3, pl.ds(z + 2 - n % 3, 1), :]
                found[n] = jnp.where(sub == j, jnp.broadcast_to(line, (TALL, LANES)), found[n])
        for n in range(27):
            gathered[n, pl.ds(pl.multiple_of(group * TALL, TALL), TALL), :] = found[n]
        return 0

    lax.fori_loop(0, rows // TALL, gather, 0, unroll=2)

    def backward(n, total):
        windows = jnp.concatenate([gathered[n * 3 + i] for i in range(3)], axis=1).astype(BF16)
        taps = jnp.concatenate([weight[n * 3 + i] for i in range(3)], axis=1)
        return total + mm_t(windows, taps)

    grad_rows[...] = lax.fori_loop(0, 9, backward, jnp.zeros((rows, channels), F32), unroll=9).astype(BF16)


def scene_kernel(
    dims,
    block0,
    block1,
    block2,
    block3,
    tiles,
    slot_rows,
    spots,
    padded,
    weight_grad,
    sent,
    slots,
    grid,
    shifted0,
    shifted1,
    acc_w,
    fetched,
    sem,
    fetch_sems,
):
    grp_count, blk_count, cap, rows, channels, size_x, size_y, size_z, scale = dims
    voxels = size_x * size_y * size_z
    devices = grp_count * blk_count
    plane = size_x * size_y
    far = (block1, block2, block3)
    fetches = [pltpu.make_async_copy(far[k], fetched.at[k], fetch_sems.at[k]) for k in range(3)]
    for fetch in fetches:
        fetch.start()
    blocks = (block0, fetched.at[0], fetched.at[1], fetched.at[2])
    each = devices // 4
    my_grp, my_blk = lax.axis_index("grp"), lax.axis_index("blk")
    me = my_grp * blk_count + my_blk
    half = me % 2

    for k, block in enumerate(blocks):

        def fill(t, _, k=k, block=block):
            s = source(me, k, t, devices)
            chosen = rows_at(voxels, slot_rows[pl.ds(s, 1), :])
            held = mm(chosen, block[t]).astype(BF16)
            g, b = s // blk_count, s % blk_count
            place = pl.ds(pl.multiple_of(b * cap, cap), cap)
            for d in range(blk_count):
                slots[g * blk_count + d, place, :] = held[d * cap : (d + 1) * cap, :]
            return 0

        if k:
            fetches[k - 1].wait()
        lax.fori_loop(0, each, fill, 0, unroll=8)

    def place_region(r, _):
        spot = spots[pl.ds(r, 1), :]
        key = spot % size_z * plane + spot // size_z
        found = mm(rows_at(voxels, key), slots[r]).astype(BF16)
        at = r % blk_count * LANES + r // blk_count * plane
        for z in range(size_z):
            grid[z, pl.ds(pl.multiple_of(at, plane), plane), :] = found[z * plane : (z + 1) * plane]
        return 0

    lax.fori_loop(0, devices, place_region, 0, unroll=16)

    def outer(dx, dy):
        g, d = my_grp + dx, my_blk + dy
        inside = (g >= 0) & (g < grp_count) & (d >= 0) & (d < blk_count)
        shape = ((1 if dx else size_x), (1 if dy else size_y), TALL, channels)
        at_x = {-1: 0, 0: 1, 1: size_x + 1}[dx]
        at_y = {-1: 0, 0: 1, 1: size_y + 1}[dy]
        there = (slice(at_x, at_x + shape[0]), slice(at_y, at_y + shape[1]))

        r = jnp.where(inside, g * blk_count + d, me)
        spot = spots[pl.ds(r, 1), :]
        key = jnp.where(inside, spot // size_z * TALL + spot % size_z + 1, -1)
        t = iota((shape[0] * shape[1] * TALL, voxels), 0)
        x0, y0 = (size_x - 1 if dx < 0 else 0), (size_y - 1 if dy < 0 else 0)
        if dy and not dx:
            want = t // TALL * (size_y * TALL) + y0 * TALL + t % TALL
        else:
            want = t + (x0 * size_y + y0) * TALL
        padded[there] = mm(one_hot(want == key), slots[r]).reshape(shape)

    for dx in (-1, 0, 1):
        for dy in (-1, 0, 1):
            outer(dx, dy)

    acc_w[...] = jnp.zeros(acc_w.shape, F32)
    offsets = ((-1, -1), (-1, 0), (-1, 1), (0, -1), (0, 0))
    sign = 1 - 2 * half
    lane = iota((LANES, LANES), 1)
    x, y = lane // size_y, lane % size_y
    nx = grp_count * size_x

    def mask(hits):
        return jnp.where(hits, 1.0, 0.0).astype(BF16)

    within, across = [], []
    for dx0, dy0 in offsets:
        dx, dy = sign * dx0, sign * dy0
        valid = (x - dx >= 0) & (x - dx < nx)
        stays = (y - dy >= 0) & (y - dy < size_y)
        within.append(mask(valid & stays))
        across.append(mask(valid & jnp.logical_not(stays)))

    def shift(z, d, there):
        def tile(dy):
            return tiles[z, :, pl.ds(pl.multiple_of((d + 1 - dy) * LANES, LANES), LANES)]

        own = tile(0)
        beside = {dy0: tile(sign * dy0) for dy0 in (-1, 1)}
        cols = pl.ds(pl.multiple_of(d * LANES, LANES), LANES)
        for m, (dx0, dy0) in enumerate(offsets):
            value = own
            if dx0 or dy0:
                ahead = sign * (dx0 * size_y + dy0)
                value = pltpu.roll(own, (ahead + LANES) % LANES, 1) * within[m]
            if dy0:
                ahead = sign * (dx0 * size_y + dy0 - dy0 * size_y)
                value = value + pltpu.roll(beside[dy0], (ahead + LANES) % LANES, 1) * across[m]
            there[m * LANES : (m + 1) * LANES, cols] = value

    def shift_first(d, _):
        shift(0, d, shifted0)
        return 0

    lax.fori_loop(0, blk_count, shift_first, 0, unroll=16)
    for z in range(size_z):
        here, there = (shifted0, shifted1) if z % 2 == 0 else (shifted1, shifted0)
        first, count = max(0, 1 - z), min(3, size_z + 1 - z) - max(0, 1 - z)
        share = -(-blk_count // count)

        def add(j, _, z=z, here=here, there=there, first=first, share=share):
            dz1 = first + j
            done = 0
            for m in range(5):
                rows_m = slice(m * LANES, (m + 1) * LANES)
                acc_w[dz1, rows_m] += mm(here[rows_m, :], grid[z + dz1 - 1])
                if z + 1 < size_z:
                    for i in range(done, share * (m + 1) // 5):
                        shift(z + 1, jnp.minimum(j * share + i, blk_count - 1), there)
                    done = share * (m + 1) // 5
            return 0

        lax.fori_loop(0, count, add, 0)

    def finish(dz1, _):
        done = (acc_w[dz1].T * scale).astype(BF16)
        for m in range(5):
            n = m + half * (4 - 2 * m)
            piece = done[:, m * LANES : (m + 1) * LANES]
            weight_grad[n * 3 + dz1] = piece
        return 0

    lax.fori_loop(0, 3, finish, 0, unroll=3)
    theirs = pltpu.make_async_copy(weight_grad.at[pl.ds(3 * half, 12)], sent, sem)
    theirs.start()
    theirs.wait()


def output_kernel(sizes, padded, weight, spots, filled, mine, received, output, weight_grad, acc_o, sems):
    half = lax.axis_index("blk") % 2
    copies = (
        pltpu.make_async_copy(mine, weight_grad.at[pl.ds(12 * half, 15)], sems.at[0]),
        pltpu.make_async_copy(received, weight_grad.at[pl.ds(15 * (1 - half), 12)], sems.at[1]),
    )
    for copy in copies:
        copy.start()
    size_x, size_y, size_z = sizes
    voxels = size_x * size_y * size_z
    plane = size_x * size_y
    channels = weight.shape[1]
    me = lax.axis_index("grp") * lax.axis_size("blk") + lax.axis_index("blk")
    acc_o[...] = jnp.zeros(acc_o.shape, F32)

    def forward(n, _):
        dx, dy = n // 3, n % 3
        window = padded[pl.ds(dx, size_x), pl.ds(dy, size_y)].reshape(plane * TALL, channels)
        taps = jnp.concatenate([weight[n * 3 + i] for i in range(3)], axis=1)
        acc_o[...] += mm(window.astype(BF16), taps)
        return 0

    lax.fori_loop(0, 9, forward, 0, unroll=9)
    spot = spots[pl.ds(me, 1), :]
    key = jnp.where(filled[pl.ds(me, 1), :] > 0, spot // size_z * TALL + spot % size_z + 1, -1)
    occupied = mm(one_hot(iota((plane * TALL, voxels), 0) == key), jnp.ones((voxels, LANES), BF16))
    total = (
        pltpu.roll(acc_o[:, 0:LANES], 1, 0)
        + acc_o[:, LANES : 2 * LANES]
        + pltpu.roll(acc_o[:, 2 * LANES :], plane * TALL - 1, 0)
    )
    rounded = (total * occupied).astype(BF16)
    row, col = iota((voxels, plane * TALL), 0), iota((voxels, plane * TALL), 1)
    squeeze = one_hot(col == row // size_z * TALL + row % size_z + 1)
    output[...] = mm(squeeze, rounded).astype(BF16)
    for copy in copies:
        copy.wait()


def exchange_masks(count):
    even = [1 << i for i in range(count.bit_length() - 2, 0, -1)]
    return even, even[1:] + even[:1]


def swap(value, count, masks):
    pairs = [(i, i ^ masks[i % 2]) for i in range(count)]
    return lax.ppermute(value, ("grp", "blk"), pairs)


def after(value, *others):
    return lax.optimization_barrier((value,) + others)[0]


def gather_all(block, count):
    even, odd = exchange_masks(count)
    held = block[None]
    for step in range(len(even) - 1):
        held = jnp.concatenate([held, swap(held, count, (even[step], odd[step]))], axis=0)
        if step == 0 and block.shape[1] == LANES:
            held = after(held)
    last = swap(held, count, (even[-1], odd[-1]))
    return held, last, swap(held, count, (1, 1)), swap(last, count, (1, 1))


def gathered_shards(features, dest, placement, weight, grad_out):
    rows, channels = features.shape
    grp_count, blk_count = lax.axis_size("grp"), lax.axis_size("blk")
    devices = grp_count * blk_count
    size_x, size_y, size_z, out_channels = grad_out.shape
    sizes = (size_x, size_y, size_z)
    voxels = size_x * size_y * size_z
    plane = size_x * size_y
    cap = voxels // blk_count
    vmem = pl.BlockSpec(memory_space=pltpu.VMEM)
    smem = pl.BlockSpec(memory_space=pltpu.SMEM)
    hbm = pl.BlockSpec(memory_space=pl.ANY)
    packed, slot = pl.pallas_call(
        functools.partial(pack_kernel, sizes, cap),
        out_shape=(
            jax.ShapeDtypeStruct((voxels + 16, LANES), BF16),
            jax.ShapeDtypeStruct((1, rows), I32),
        ),
        in_specs=[vmem] * 3,
        out_specs=(vmem, vmem),
        name="pack",
    )(dest.reshape(1, rows), placement, grad_out.reshape(voxels, out_channels))
    cotangents = gather_all(packed, devices)
    cells = gather_all(features, devices)
    dims = (grp_count, blk_count, cap, rows, channels) + sizes
    grad_rows, tiles, slot_rows, spots, filled = pl.pallas_call(
        functools.partial(cotangent_kernel, dims),
        out_shape=(
            jax.ShapeDtypeStruct((rows, channels), BF16),
            jax.ShapeDtypeStruct((size_z, out_channels, (blk_count + 2) * LANES), BF16),
            jax.ShapeDtypeStruct((devices, rows), I32),
            jax.ShapeDtypeStruct((devices, voxels), I32),
            jax.ShapeDtypeStruct((devices, voxels), F32),
        ),
        in_specs=[smem, vmem] + [hbm] * 3 + [vmem],
        out_specs=(vmem,) * 5,
        scratch_shapes=[
            pltpu.VMEM((size_x + 2, blk_count * size_y + 2, TALL, out_channels), F32),
            pltpu.VMEM((27, rows, out_channels), F32),
            pltpu.VMEM((grp_count, plane * TALL, voxels), BF16),
            pltpu.VMEM((devices, LANES), F32),
            pltpu.VMEM((devices, voxels), F32),
            pltpu.VMEM((devices, out_channels, voxels), BF16),
            pltpu.VMEM((3,) + cotangents[0].shape, BF16),
            pltpu.SMEM((blk_count, voxels), I32),
            pltpu.SemaphoreType.DMA,
            pltpu.SemaphoreType.DMA((3,)),
        ],
        compiler_params=pltpu.CompilerParams(vmem_limit_bytes=24 * 1024 * 1024),
        name="cotangent",
    )(slot, *cotangents, weight)
    scale = 1.0 / math.sqrt(rows * devices)
    padded, some, sent = pl.pallas_call(
        functools.partial(scene_kernel, dims + (scale,)),
        out_shape=(
            jax.ShapeDtypeStruct((size_x + 2, size_y + 2, TALL, channels), F32),
            jax.ShapeDtypeStruct((15, channels, out_channels), BF16),
            jax.ShapeDtypeStruct((12, channels, out_channels), BF16),
        ),
        in_specs=[vmem] + [hbm] * 3 + [vmem] * 3,
        out_specs=(vmem, vmem, hbm),
        scratch_shapes=[
            pltpu.VMEM((devices, voxels, channels), BF16),
            pltpu.VMEM((size_z, blk_count * LANES, channels), BF16),
            pltpu.VMEM((5 * out_channels, blk_count * LANES), BF16),
            pltpu.VMEM((5 * out_channels, blk_count * LANES), BF16),
            pltpu.VMEM((3, 5 * out_channels, channels), F32),
            pltpu.VMEM((3,) + cells[0].shape, BF16),
            pltpu.SemaphoreType.DMA,
            pltpu.SemaphoreType.DMA((3,)),
        ],
        compiler_params=pltpu.CompilerParams(vmem_limit_bytes=24 * 1024 * 1024),
        name="scene",
    )(*cells, tiles, slot_rows, spots)
    received = swap(sent, devices, (1, 1))
    output, weight_grad = pl.pallas_call(
        functools.partial(output_kernel, sizes),
        out_shape=(
            jax.ShapeDtypeStruct((voxels, out_channels), BF16),
            jax.ShapeDtypeStruct(weight.shape, BF16),
        ),
        in_specs=[vmem] * 6,
        out_specs=(vmem, hbm),
        scratch_shapes=[
            pltpu.VMEM((plane * TALL, 3 * out_channels), F32),
            pltpu.SemaphoreType.DMA((2,)),
        ],
        compiler_params=pltpu.CompilerParams(vmem_limit_bytes=12 * 1024 * 1024),
        name="output",
    )(padded, weight, spots, filled, some, received)
    return output.reshape(grad_out.shape), grad_rows, weight_grad


def extended(cells, sides, width):
    for axis, dim in sides:
        count = lax.axis_size(axis)
        ends = count - 1
        head = lax.slice_in_dim(cells, 0, width, axis=dim)
        tail = lax.slice_in_dim(cells, cells.shape[dim] - width, cells.shape[dim], axis=dim)
        cells = jnp.concatenate(
            [
                lax.ppermute(tail, axis, [(i, (i + 1) % count) for i in range(ends)]),
                cells,
                lax.ppermute(head, axis, [((i + 1) % count, i) for i in range(ends)]),
            ],
            axis=dim,
        )
    return cells


def summed_shards(features, dest, placement, weight, grad_out):
    row_count, channels = features.shape
    blk_count = lax.axis_size("blk")
    grp_count = lax.axis_size("grp")
    voxel_of_slot = placement[0]
    voxel_count = voxel_of_slot.shape[0]
    capacity = voxel_count // blk_count
    size_x, size_y, size_z, out_channels = grad_out.shape
    target = dest[:, 0]
    owners = jnp.arange(blk_count, dtype=jnp.int32)
    one_hot = (target[:, None] == owners[None, :]).astype(jnp.int32)
    slot_rank = jnp.sum((jnp.cumsum(one_hot, axis=0) - one_hot) * one_hot, axis=1)
    send_counts = jnp.sum(one_hot, axis=0).reshape(blk_count, 1)
    slot_index = target * capacity + slot_rank
    outgoing = jnp.zeros((voxel_count, channels), jnp.bfloat16).at[slot_index].set(features)
    incoming, recv_counts = (
        lax.all_to_all(
            outgoing.reshape(blk_count, capacity, channels),
            "blk",
            split_axis=0,
            concat_axis=0,
            tiled=True,
        ),
        lax.all_to_all(send_counts, "blk", split_axis=0, concat_axis=0, tiled=True),
    )
    filled = (
        (jnp.arange(capacity, dtype=jnp.int32)[None, :] < recv_counts)
        .reshape(-1)
        .astype(jnp.float32)
    )
    voxel_rows = (
        jnp.zeros((voxel_count, channels), jnp.bfloat16)
        .at[voxel_of_slot]
        .set(incoming.reshape(voxel_count, channels))
    )
    occupied = jnp.zeros((voxel_count,), jnp.float32).at[voxel_of_slot].set(filled)[:, None]
    voxel_grid = voxel_rows.reshape(size_x, size_y, size_z, channels)
    padded = extended(voxel_grid, (("grp", 0), ("blk", 1)), 1)
    padded = jnp.pad(padded, ((0, 0), (0, 0), (1, 1), (0, 0)))
    shifted = []
    total = jnp.zeros((voxel_count, out_channels), jnp.float32)
    for offset in range(27):
        shift_x, shift_y, shift_z = (offset // 9, offset // 3 % 3, offset % 3)
        window = padded[
            shift_x : shift_x + size_x, shift_y : shift_y + size_y, shift_z : shift_z + size_z
        ].reshape(voxel_count, channels)
        shifted.append(window)
        total = total + jnp.dot(window, weight[offset], preferred_element_type=jnp.float32)
    output = (total * occupied).astype(jnp.bfloat16).reshape(size_x, size_y, size_z, out_channels)
    masked_grad = (
        grad_out.reshape(voxel_count, out_channels).astype(jnp.float32) * occupied
    ).astype(jnp.bfloat16)
    grad_padded = extended(
        masked_grad.reshape(size_x, size_y, size_z, out_channels), (("grp", 0), ("blk", 1)), 1
    )
    grad_padded = jnp.pad(grad_padded, ((0, 0), (0, 0), (1, 1), (0, 0)))
    back_total = jnp.zeros((voxel_count, channels), jnp.float32)
    partials = []
    for offset in range(27):
        shift_x, shift_y, shift_z = (offset // 9, offset // 3 % 3, offset % 3)
        window = grad_padded[
            2 - shift_x : 2 - shift_x + size_x,
            2 - shift_y : 2 - shift_y + size_y,
            2 - shift_z : 2 - shift_z + size_z,
        ].reshape(voxel_count, out_channels)
        back_total = back_total + lax.dot_general(
            window, weight[offset], (((1,), (1,)), ((), ())), preferred_element_type=jnp.float32
        )
        partials.append(
            lax.dot_general(
                shifted[offset],
                masked_grad,
                (((0,), (0,)), ((), ())),
                preferred_element_type=jnp.float32,
            )
        )
    grad_grid = (back_total * occupied).astype(jnp.bfloat16)
    weight_terms = jnp.stack(partials).reshape(27 * channels, out_channels)
    grad_scale = 1.0 / math.sqrt(row_count * blk_count * grp_count)
    weight_grad = (lax.psum(weight_terms, ("grp", "blk")) * grad_scale).astype(jnp.bfloat16)
    weight_grad = weight_grad.reshape(27, channels, out_channels)
    returning = grad_grid[voxel_of_slot].reshape(blk_count, capacity, channels)
    returned = lax.all_to_all(returning, "blk", split_axis=0, concat_axis=0, tiled=True)
    grad_rows = returned.reshape(voxel_count, channels)[slot_index]
    return (output, grad_rows, weight_grad)


def fits(mesh):
    grp_count, blk_count = mesh.shape["grp"], mesh.shape["blk"]
    return blk_count == 16 and grp_count == 2


def solution(mesh):
    in_specs = (
        P(("grp", "blk"), None),
        P(("grp", "blk"), None),
        P(("grp", "blk"), None),
        P(),
        P("grp", "blk", None, None),
    )
    out_specs = (P("grp", "blk", None, None), P(("grp", "blk"), None), P())
    shards = gathered_shards if fits(mesh) else summed_shards
    return jax.shard_map(shards, mesh=mesh, in_specs=in_specs, out_specs=out_specs, check_vma=False)
```

```python
import functools
import math

import jax
import jax.numpy as jnp
from jax import lax
from jax.experimental import pallas as pl
from jax.experimental.pallas import tpu as pltpu
from jax.sharding import PartitionSpec as P

LANES = 128
TALL = 8
F32, BF16, I32 = jnp.float32, jnp.bfloat16, jnp.int32


def iota(shape, axis):
    return lax.broadcasted_iota(I32, shape, axis)


def one_hot(hits):
    return jnp.where(hits, 1.0, 0.0).astype(BF16)


def rows_at(count, key):
    shape = (count, key.shape[1])
    places = iota(shape, 0).astype(BF16)
    return jnp.where(places == jnp.broadcast_to(key.astype(BF16), shape), 1.0, 0.0).astype(BF16)


def mm(a, b):
    return lax.dot_general(a, b, (((1,), (0,)), ((), ())), preferred_element_type=F32)


def mm_t(a, b):
    return lax.dot_general(a, b, (((1,), (1,)), ((), ())), preferred_element_type=F32)


def half_order(z, flat, group, plane):
    return z // 2 * (2 * plane) + (z + group) % 2 * plane + flat


def pack_kernel(sizes, cap, dest, placement, grad, packed, slots):
    size_x, size_y, size_z = sizes
    rows = dest.shape[1]
    voxels = grad.shape[0]
    plane = size_x * size_y
    lane = iota((rows, LANES), 1)
    upright = iota((rows, rows), 0) == iota((rows, rows), 1)
    target = jnp.sum(jnp.where(upright, dest[...], 0), axis=1, keepdims=True)
    named = one_hot(lane == target)
    earlier = one_hot(iota((rows, rows), 0) > iota((rows, rows), 1))
    rank = jnp.sum(mm(earlier, named) * named.astype(F32), axis=1, keepdims=True)
    slot = target.astype(F32) * cap + rank
    slot_row = jnp.sum(jnp.where(upright, slot, 0.0), axis=0, keepdims=True)
    counts = jnp.sum(named.astype(F32), axis=0, keepdims=True)
    slots[...] = slot_row.astype(I32)
    row, col = iota((voxels, voxels), 0), iota((voxels, voxels), 1)
    moved = half_order(row % size_z, row // size_z, lax.axis_index("grp"), plane)
    turned = mm(grad[...].astype(F32).T.astype(BF16), one_hot(col == moved)).astype(BF16)
    halves = voxels // LANES
    for h in range(halves):
        packed[h * LANES : (h + 1) * LANES, :] = turned[:, h * LANES : (h + 1) * LANES]
    spots = placement[...].astype(F32)
    index_rows = [slot_row, counts] + [spots[:, h * LANES : (h + 1) * LANES] for h in range(halves)]
    index_rows.append(jnp.zeros((16 - len(index_rows), LANES), F32))
    packed[halves * LANES : halves * LANES + 16, :] = jnp.concatenate(index_rows, axis=0).astype(BF16)


def source(me, buffer, t, count):
    even, odd = exchange_masks(count)

    def apart(masks):
        total = masks[-1] * (buffer % 2)
        for i in range(len(masks) - 1):
            total = total + (t >> i) % 2 * masks[i]
        return total

    holder = me ^ (buffer // 2)
    return holder ^ jnp.where(holder % 2 == 0, apart(even), apart(odd))


def cotangent_kernel(
    dims,
    slot_ref,
    block0,
    block1,
    block2,
    block3,
    weight,
    grad_rows,
    tiles,
    slot_rows,
    spots,
    filled,
    padded,
    gathered,
    stretch,
    counts,
    occupied,
    masked,
    fetched,
    spots_s,
    sem,
    fetch_sems,
):
    grp_count, blk_count, cap, rows, channels, size_x, size_y, size_z = dims
    voxels = size_x * size_y * size_z
    devices = grp_count * blk_count
    plane = size_x * size_y
    halves = voxels // LANES
    far = (block1, block2, block3)
    fetches = [pltpu.make_async_copy(far[k], fetched.at[k], fetch_sems.at[k]) for k in range(3)]
    for fetch in fetches:
        fetch.start()
    blocks = (block0, fetched.at[0], fetched.at[1], fetched.at[2])
    each = devices // 4
    my_grp, my_blk = lax.axis_index("grp"), lax.axis_index("blk")
    me = my_grp * blk_count + my_blk

    for g in range(grp_count):
        row, col = iota((plane * TALL, voxels), 0), iota((plane * TALL, voxels), 1)
        z = row % TALL - 1
        inside = (z >= 0) & (z < size_z)
        stretch[g] = one_hot(inside & (col == half_order(z, row // TALL, g, plane)))

    zero_plane = jnp.zeros((1,) + padded.shape[1:], F32)
    zero_line = jnp.zeros((padded.shape[0], 1) + padded.shape[2:], F32)

    @pl.when(my_grp == 0)
    def _():
        padded[0:1] = zero_plane

    @pl.when(my_grp == grp_count - 1)
    def _():
        padded[size_x + 1 : size_x + 2] = zero_plane

    padded[:, 0:1] = zero_line
    padded[:, padded.shape[1] - 1 :] = zero_line
    for z in range(size_z):
        tiles[z, :, 0:LANES] = jnp.zeros((LANES, LANES), BF16)
        tiles[z, :, (blk_count + 1) * LANES :] = jnp.zeros((LANES, LANES), BF16)

    for k, block in enumerate(blocks):

        def read(t, _, k=k, block=block):
            s = source(me, k, t, devices)
            index = block[t, halves * LANES : halves * LANES + 16, :].astype(F32)
            slot_rows[pl.ds(s, 1), :] = index[0:1].astype(I32)
            counts[pl.ds(s, 1), :] = index[1:2]
            row = jnp.concatenate([index[2 + h : 3 + h] for h in range(halves)], axis=1)
            spots[pl.ds(s, 1), :] = row.astype(I32)
            return 0

        if k:
            fetches[k - 1].wait()
        lax.fori_loop(0, each, read, 0, unroll=8)
    copy = pltpu.make_async_copy(
        spots.at[pl.ds(pl.multiple_of(my_grp * blk_count, blk_count), blk_count)], spots_s, sem
    )
    copy.start()

    spread = one_hot(iota((blk_count, voxels), 0) == iota((blk_count, voxels), 1) // cap)
    rank = (iota((blk_count, voxels), 1) % cap).astype(F32)
    for g in range(grp_count):
        sent = counts[g * blk_count : (g + 1) * blk_count, :].T[:blk_count].astype(BF16)
        held = jnp.where(rank < mm(sent, spread), 1.0, 0.0)
        filled[g * blk_count : (g + 1) * blk_count, :] = held

    def occupy(r, _):
        spot = spots[pl.ds(r, 1), :]
        key = half_order(spot % size_z, spot // size_z, r // blk_count, plane)
        held = jnp.broadcast_to(filled[pl.ds(r, 1), :], (16, voxels)).astype(BF16)
        occupied[pl.ds(r, 1), :] = mm_t(held, rows_at(voxels, key))[0:1]
        return 0

    lax.fori_loop(0, devices, occupy, 0, unroll=32)

    for k, block in enumerate(blocks):

        def mask(t, _, k=k, block=block):
            r = source(me, k, t, devices)
            there = occupied[pl.ds(r, 1), :].astype(BF16)
            for h in range(halves):
                at = slice(h * LANES, (h + 1) * LANES)
                masked[r, :, at] = block[t, at, :] * there[:, at]
            return 0

        lax.fori_loop(0, each, mask, 0, unroll=8)

    first = iota((LANES, LANES), 1) < plane

    def tile(d, _):
        cols = pl.ds(pl.multiple_of((d + 1) * LANES, LANES), LANES)
        for h in range(halves):
            at = slice(h * LANES, (h + 1) * LANES)
            left, right = masked[d, :, at], masked[blk_count + d, :, at]
            tiles[2 * h, :, cols] = jnp.where(first, left, right)
            tiles[2 * h + 1, :, cols] = pltpu.roll(jnp.where(first, right, left), plane, 1)
        return 0

    lax.fori_loop(0, blk_count, tile, 0, unroll=8)

    def stand(d, _):
        found = mm_t(stretch[my_grp], masked[my_grp * blk_count + d])
        padded[1 : size_x + 1, pl.ds(d * size_y + 1, size_y)] = found.reshape(size_x, size_y, TALL, LANES)
        return 0

    lax.fori_loop(0, blk_count, stand, 0, unroll=8)

    near = 1 - my_grp
    lines = pl.ds(pl.multiple_of(jnp.where(my_grp == 0, 0, size_x - 1) * size_y * TALL, size_y * TALL), size_y * TALL)

    def stand_near(d, _):
        found = mm_t(stretch[near, lines, :], masked[near * blk_count + d])
        at_x = pl.ds(jnp.where(my_grp == 0, size_x + 1, 0), 1)
        padded[at_x, pl.ds(d * size_y + 1, size_y)] = found.reshape(1, size_y, TALL, LANES)
        return 0

    lax.fori_loop(0, blk_count, stand_near, 0, unroll=16)

    copy.wait()
    sub = iota((TALL, LANES), 0)

    def gather(group, _):
        found = [jnp.zeros((TALL, LANES), F32)] * 27
        for j in range(TALL):
            slot = slot_ref[0, group * TALL + j]
            d = slot // cap
            v = spots_s[d, my_blk * cap + slot % cap]
            x, y, z = v // (size_y * size_z), d * size_y + v // size_z % size_y, v % size_z
            for n in range(27):
                line = padded[x + 2 - n // 9, y + 2 - n // 3 % 3, pl.ds(z + 2 - n % 3, 1), :]
                found[n] = jnp.where(sub == j, jnp.broadcast_to(line, (TALL, LANES)), found[n])
        for n in range(27):
            gathered[n, pl.ds(pl.multiple_of(group * TALL, TALL), TALL), :] = found[n]
        return 0

    lax.fori_loop(0, rows // TALL, gather, 0, unroll=2)

    def backward(n, total):
        windows = jnp.concatenate([gathered[n * 3 + i] for i in range(3)], axis=1).astype(BF16)
        taps = jnp.concatenate([weight[n * 3 + i] for i in range(3)], axis=1)
        return total + mm_t(windows, taps)

    grad_rows[...] = lax.fori_loop(0, 9, backward, jnp.zeros((rows, channels), F32), unroll=9).astype(BF16)


def scene_kernel(
    dims,
    block0,
    block1,
    block2,
    block3,
    tiles,
    slot_rows,
    spots,
    padded,
    weight_grad,
    sent,
    slots,
    grid,
    shifted0,
    shifted1,
    acc_w,
    fetched,
    sem,
    fetch_sems,
):
    grp_count, blk_count, cap, rows, channels, size_x, size_y, size_z, scale = dims
    voxels = size_x * size_y * size_z
    devices = grp_count * blk_count
    plane = size_x * size_y
    far = (block1, block2, block3)
    fetches = [pltpu.make_async_copy(far[k], fetched.at[k], fetch_sems.at[k]) for k in range(3)]
    for fetch in fetches:
        fetch.start()
    blocks = (block0, fetched.at[0], fetched.at[1], fetched.at[2])
    each = devices // 4
    my_grp, my_blk = lax.axis_index("grp"), lax.axis_index("blk")
    me = my_grp * blk_count + my_blk
    half = me % 2

    for k, block in enumerate(blocks):

        def fill(t, _, k=k, block=block):
            s = source(me, k, t, devices)
            chosen = rows_at(voxels, slot_rows[pl.ds(s, 1), :])
            held = mm(chosen, block[t]).astype(BF16)
            g, b = s // blk_count, s % blk_count
            place = pl.ds(pl.multiple_of(b * cap, cap), cap)
            for d in range(blk_count):
                slots[g * blk_count + d, place, :] = held[d * cap : (d + 1) * cap, :]
            return 0

        if k:
            fetches[k - 1].wait()
        lax.fori_loop(0, each, fill, 0, unroll=8)

    def place_region(r, _):
        spot = spots[pl.ds(r, 1), :]
        key = spot % size_z * plane + spot // size_z
        found = mm(rows_at(voxels, key), slots[r]).astype(BF16)
        at = r % blk_count * LANES + r // blk_count * plane
        for z in range(size_z):
            grid[z, pl.ds(pl.multiple_of(at, plane), plane), :] = found[z * plane : (z + 1) * plane]
        return 0

    lax.fori_loop(0, devices, place_region, 0, unroll=16)

    def outer(dx, dy):
        g, d = my_grp + dx, my_blk + dy
        inside = (g >= 0) & (g < grp_count) & (d >= 0) & (d < blk_count)
        shape = ((1 if dx else size_x), (1 if dy else size_y), TALL, channels)
        at_x = {-1: 0, 0: 1, 1: size_x + 1}[dx]
        at_y = {-1: 0, 0: 1, 1: size_y + 1}[dy]
        there = (slice(at_x, at_x + shape[0]), slice(at_y, at_y + shape[1]))

        r = jnp.where(inside, g * blk_count + d, me)
        spot = spots[pl.ds(r, 1), :]
        key = jnp.where(inside, spot // size_z * TALL + spot % size_z + 1, -1)
        t = iota((shape[0] * shape[1] * TALL, voxels), 0)
        x0, y0 = (size_x - 1 if dx < 0 else 0), (size_y - 1 if dy < 0 else 0)
        if dy and not dx:
            want = t // TALL * (size_y * TALL) + y0 * TALL + t % TALL
        else:
            want = t + (x0 * size_y + y0) * TALL
        padded[there] = mm(one_hot(want == key), slots[r]).reshape(shape)

    for dx in (-1, 0, 1):
        for dy in (-1, 0, 1):
            outer(dx, dy)

    acc_w[...] = jnp.zeros(acc_w.shape, F32)
    offsets = ((-1, -1), (-1, 0), (-1, 1), (0, -1), (0, 0))
    sign = 1 - 2 * half
    lane = iota((LANES, LANES), 1)
    x, y = lane // size_y, lane % size_y
    nx = grp_count * size_x

    def mask(hits):
        return jnp.where(hits, 1.0, 0.0).astype(BF16)

    within, across = [], []
    for dx0, dy0 in offsets:
        dx, dy = sign * dx0, sign * dy0
        valid = (x - dx >= 0) & (x - dx < nx)
        stays = (y - dy >= 0) & (y - dy < size_y)
        within.append(mask(valid & stays))
        across.append(mask(valid & jnp.logical_not(stays)))

    def shift(z, d, there):
        def tile(dy):
            return tiles[z, :, pl.ds(pl.multiple_of((d + 1 - dy) * LANES, LANES), LANES)]

        own = tile(0)
        beside = {dy0: tile(sign * dy0) for dy0 in (-1, 1)}
        cols = pl.ds(pl.multiple_of(d * LANES, LANES), LANES)
        for m, (dx0, dy0) in enumerate(offsets):
            value = own
            if dx0 or dy0:
                ahead = sign * (dx0 * size_y + dy0)
                value = pltpu.roll(own, (ahead + LANES) % LANES, 1) * within[m]
            if dy0:
                ahead = sign * (dx0 * size_y + dy0 - dy0 * size_y)
                value = value + pltpu.roll(beside[dy0], (ahead + LANES) % LANES, 1) * across[m]
            there[m * LANES : (m + 1) * LANES, cols] = value

    def shift_first(d, _):
        shift(0, d, shifted0)
        return 0

    lax.fori_loop(0, blk_count, shift_first, 0, unroll=16)
    for z in range(size_z):
        here, there = (shifted0, shifted1) if z % 2 == 0 else (shifted1, shifted0)
        first, count = max(0, 1 - z), min(3, size_z + 1 - z) - max(0, 1 - z)
        share = -(-blk_count // count)

        def add(j, _, z=z, here=here, there=there, first=first, share=share):
            dz1 = first + j
            done = 0
            for m in range(5):
                rows_m = slice(m * LANES, (m + 1) * LANES)
                acc_w[dz1, rows_m] += mm(here[rows_m, :], grid[z + dz1 - 1])
                if z + 1 < size_z:
                    for i in range(done, share * (m + 1) // 5):
                        shift(z + 1, jnp.minimum(j * share + i, blk_count - 1), there)
                    done = share * (m + 1) // 5
            return 0

        lax.fori_loop(0, count, add, 0)

    def finish(dz1, _):
        done = (acc_w[dz1].T * scale).astype(BF16)
        for m in range(5):
            n = m + half * (4 - 2 * m)
            piece = done[:, m * LANES : (m + 1) * LANES]
            weight_grad[n * 3 + dz1] = piece
        return 0

    lax.fori_loop(0, 3, finish, 0, unroll=3)
    theirs = pltpu.make_async_copy(weight_grad.at[pl.ds(3 * half, 12)], sent, sem)
    theirs.start()
    theirs.wait()


def output_kernel(sizes, padded, weight, spots, filled, mine, received, output, weight_grad, acc_o, sems):
    half = lax.axis_index("blk") % 2
    copies = (
        pltpu.make_async_copy(mine, weight_grad.at[pl.ds(12 * half, 15)], sems.at[0]),
        pltpu.make_async_copy(received, weight_grad.at[pl.ds(15 * (1 - half), 12)], sems.at[1]),
    )
    for copy in copies:
        copy.start()
    size_x, size_y, size_z = sizes
    voxels = size_x * size_y * size_z
    plane = size_x * size_y
    channels = weight.shape[1]
    me = lax.axis_index("grp") * lax.axis_size("blk") + lax.axis_index("blk")
    acc_o[...] = jnp.zeros(acc_o.shape, F32)

    def forward(n, _):
        dx, dy = n // 3, n % 3
        window = padded[pl.ds(dx, size_x), pl.ds(dy, size_y)].reshape(plane * TALL, channels)
        taps = jnp.concatenate([weight[n * 3 + i] for i in range(3)], axis=1)
        acc_o[...] += mm(window.astype(BF16), taps)
        return 0

    lax.fori_loop(0, 9, forward, 0, unroll=9)
    spot = spots[pl.ds(me, 1), :]
    key = jnp.where(filled[pl.ds(me, 1), :] > 0, spot // size_z * TALL + spot % size_z + 1, -1)
    occupied = mm(one_hot(iota((plane * TALL, voxels), 0) == key), jnp.ones((voxels, LANES), BF16))
    total = (
        pltpu.roll(acc_o[:, 0:LANES], 1, 0)
        + acc_o[:, LANES : 2 * LANES]
        + pltpu.roll(acc_o[:, 2 * LANES :], plane * TALL - 1, 0)
    )
    rounded = (total * occupied).astype(BF16)
    row, col = iota((voxels, plane * TALL), 0), iota((voxels, plane * TALL), 1)
    squeeze = one_hot(col == row // size_z * TALL + row % size_z + 1)
    output[...] = mm(squeeze, rounded).astype(BF16)
    for copy in copies:
        copy.wait()


def exchange_masks(count):
    far, mid, near, last = (count >> i for i in range(1, 5))
    return (mid, far, near, last), (near, mid, last, far)


def swap(value, count, masks):
    pairs = [(i, i ^ masks[i % 2]) for i in range(count)]
    return lax.ppermute(value, ("grp", "blk"), pairs)


def after(value, *others):
    return lax.optimization_barrier((value,) + others)[0]


def gather_all(block, count):
    even, odd = exchange_masks(count)
    held = block[None]
    for step in range(len(even) - 1):
        held = jnp.concatenate([held, swap(held, count, (even[step], odd[step]))], axis=0)
        if step == 0 and block.shape[1] == LANES:
            held = after(held)
    last = swap(held, count, (even[-1], odd[-1]))
    return held, last, swap(held, count, (1, 1)), swap(last, count, (1, 1))


def gathered_shards(features, dest, placement, weight, grad_out):
    rows, channels = features.shape
    grp_count, blk_count = lax.axis_size("grp"), lax.axis_size("blk")
    devices = grp_count * blk_count
    size_x, size_y, size_z, out_channels = grad_out.shape
    sizes = (size_x, size_y, size_z)
    voxels = size_x * size_y * size_z
    plane = size_x * size_y
    cap = voxels // blk_count
    vmem = pl.BlockSpec(memory_space=pltpu.VMEM)
    smem = pl.BlockSpec(memory_space=pltpu.SMEM)
    hbm = pl.BlockSpec(memory_space=pl.ANY)
    packed, slot = pl.pallas_call(
        functools.partial(pack_kernel, sizes, cap),
        out_shape=(
            jax.ShapeDtypeStruct((voxels + 16, LANES), BF16),
            jax.ShapeDtypeStruct((1, rows), I32),
        ),
        in_specs=[vmem] * 3,
        out_specs=(vmem, vmem),
        name="pack",
    )(dest.reshape(1, rows), placement, grad_out.reshape(voxels, out_channels))
    cotangents = gather_all(packed, devices)
    cells = gather_all(features, devices)
    dims = (grp_count, blk_count, cap, rows, channels) + sizes
    grad_rows, tiles, slot_rows, spots, filled = pl.pallas_call(
        functools.partial(cotangent_kernel, dims),
        out_shape=(
            jax.ShapeDtypeStruct((rows, channels), BF16),
            jax.ShapeDtypeStruct((size_z, out_channels, (blk_count + 2) * LANES), BF16),
            jax.ShapeDtypeStruct((devices, rows), I32),
            jax.ShapeDtypeStruct((devices, voxels), I32),
            jax.ShapeDtypeStruct((devices, voxels), F32),
        ),
        in_specs=[smem, vmem] + [hbm] * 3 + [vmem],
        out_specs=(vmem,) * 5,
        scratch_shapes=[
            pltpu.VMEM((size_x + 2, blk_count * size_y + 2, TALL, out_channels), F32),
            pltpu.VMEM((27, rows, out_channels), F32),
            pltpu.VMEM((grp_count, plane * TALL, voxels), BF16),
            pltpu.VMEM((devices, LANES), F32),
            pltpu.VMEM((devices, voxels), F32),
            pltpu.VMEM((devices, out_channels, voxels), BF16),
            pltpu.VMEM((3,) + cotangents[0].shape, BF16),
            pltpu.SMEM((blk_count, voxels), I32),
            pltpu.SemaphoreType.DMA,
            pltpu.SemaphoreType.DMA((3,)),
        ],
        compiler_params=pltpu.CompilerParams(vmem_limit_bytes=24 * 1024 * 1024),
        name="cotangent",
    )(slot, *cotangents, weight)
    scale = 1.0 / math.sqrt(rows * devices)
    padded, some, sent = pl.pallas_call(
        functools.partial(scene_kernel, dims + (scale,)),
        out_shape=(
            jax.ShapeDtypeStruct((size_x + 2, size_y + 2, TALL, channels), F32),
            jax.ShapeDtypeStruct((15, channels, out_channels), BF16),
            jax.ShapeDtypeStruct((12, channels, out_channels), BF16),
        ),
        in_specs=[vmem] + [hbm] * 3 + [vmem] * 3,
        out_specs=(vmem, vmem, hbm),
        scratch_shapes=[
            pltpu.VMEM((devices, voxels, channels), BF16),
            pltpu.VMEM((size_z, blk_count * LANES, channels), BF16),
            pltpu.VMEM((5 * out_channels, blk_count * LANES), BF16),
            pltpu.VMEM((5 * out_channels, blk_count * LANES), BF16),
            pltpu.VMEM((3, 5 * out_channels, channels), F32),
            pltpu.VMEM((3,) + cells[0].shape, BF16),
            pltpu.SemaphoreType.DMA,
            pltpu.SemaphoreType.DMA((3,)),
        ],
        compiler_params=pltpu.CompilerParams(vmem_limit_bytes=24 * 1024 * 1024),
        name="scene",
    )(*cells, tiles, slot_rows, spots)
    received = swap(sent, devices, (1, 1))
    output, weight_grad = pl.pallas_call(
        functools.partial(output_kernel, sizes),
        out_shape=(
            jax.ShapeDtypeStruct((voxels, out_channels), BF16),
            jax.ShapeDtypeStruct(weight.shape, BF16),
        ),
        in_specs=[vmem] * 6,
        out_specs=(vmem, hbm),
        scratch_shapes=[
            pltpu.VMEM((plane * TALL, 3 * out_channels), F32),
            pltpu.SemaphoreType.DMA((2,)),
        ],
        compiler_params=pltpu.CompilerParams(vmem_limit_bytes=12 * 1024 * 1024),
        name="output",
    )(padded, weight, spots, filled, some, received)
    return output.reshape(grad_out.shape), grad_rows, weight_grad


def extended(cells, sides, width):
    for axis, dim in sides:
        count = lax.axis_size(axis)
        ends = count - 1
        head = lax.slice_in_dim(cells, 0, width, axis=dim)
        tail = lax.slice_in_dim(cells, cells.shape[dim] - width, cells.shape[dim], axis=dim)
        cells = jnp.concatenate(
            [
                lax.ppermute(tail, axis, [(i, (i + 1) % count) for i in range(ends)]),
                cells,
                lax.ppermute(head, axis, [((i + 1) % count, i) for i in range(ends)]),
            ],
            axis=dim,
        )
    return cells


def summed_shards(features, dest, placement, weight, grad_out):
    row_count, channels = features.shape
    blk_count = lax.axis_size("blk")
    grp_count = lax.axis_size("grp")
    voxel_of_slot = placement[0]
    voxel_count = voxel_of_slot.shape[0]
    capacity = voxel_count // blk_count
    size_x, size_y, size_z, out_channels = grad_out.shape
    target = dest[:, 0]
    owners = jnp.arange(blk_count, dtype=jnp.int32)
    one_hot = (target[:, None] == owners[None, :]).astype(jnp.int32)
    slot_rank = jnp.sum((jnp.cumsum(one_hot, axis=0) - one_hot) * one_hot, axis=1)
    send_counts = jnp.sum(one_hot, axis=0).reshape(blk_count, 1)
    slot_index = target * capacity + slot_rank
    outgoing = jnp.zeros((voxel_count, channels), jnp.bfloat16).at[slot_index].set(features)
    incoming, recv_counts = (
        lax.all_to_all(
            outgoing.reshape(blk_count, capacity, channels),
            "blk",
            split_axis=0,
            concat_axis=0,
            tiled=True,
        ),
        lax.all_to_all(send_counts, "blk", split_axis=0, concat_axis=0, tiled=True),
    )
    filled = (
        (jnp.arange(capacity, dtype=jnp.int32)[None, :] < recv_counts)
        .reshape(-1)
        .astype(jnp.float32)
    )
    voxel_rows = (
        jnp.zeros((voxel_count, channels), jnp.bfloat16)
        .at[voxel_of_slot]
        .set(incoming.reshape(voxel_count, channels))
    )
    occupied = jnp.zeros((voxel_count,), jnp.float32).at[voxel_of_slot].set(filled)[:, None]
    voxel_grid = voxel_rows.reshape(size_x, size_y, size_z, channels)
    padded = extended(voxel_grid, (("grp", 0), ("blk", 1)), 1)
    padded = jnp.pad(padded, ((0, 0), (0, 0), (1, 1), (0, 0)))
    shifted = []
    total = jnp.zeros((voxel_count, out_channels), jnp.float32)
    for offset in range(27):
        shift_x, shift_y, shift_z = (offset // 9, offset // 3 % 3, offset % 3)
        window = padded[
            shift_x : shift_x + size_x, shift_y : shift_y + size_y, shift_z : shift_z + size_z
        ].reshape(voxel_count, channels)
        shifted.append(window)
        total = total + jnp.dot(window, weight[offset], preferred_element_type=jnp.float32)
    output = (total * occupied).astype(jnp.bfloat16).reshape(size_x, size_y, size_z, out_channels)
    masked_grad = (
        grad_out.reshape(voxel_count, out_channels).astype(jnp.float32) * occupied
    ).astype(jnp.bfloat16)
    grad_padded = extended(
        masked_grad.reshape(size_x, size_y, size_z, out_channels), (("grp", 0), ("blk", 1)), 1
    )
    grad_padded = jnp.pad(grad_padded, ((0, 0), (0, 0), (1, 1), (0, 0)))
    back_total = jnp.zeros((voxel_count, channels), jnp.float32)
    partials = []
    for offset in range(27):
        shift_x, shift_y, shift_z = (offset // 9, offset // 3 % 3, offset % 3)
        window = grad_padded[
            2 - shift_x : 2 - shift_x + size_x,
            2 - shift_y : 2 - shift_y + size_y,
            2 - shift_z : 2 - shift_z + size_z,
        ].reshape(voxel_count, out_channels)
        back_total = back_total + lax.dot_general(
            window, weight[offset], (((1,), (1,)), ((), ())), preferred_element_type=jnp.float32
        )
        partials.append(
            lax.dot_general(
                shifted[offset],
                masked_grad,
                (((0,), (0,)), ((), ())),
                preferred_element_type=jnp.float32,
            )
        )
    grad_grid = (back_total * occupied).astype(jnp.bfloat16)
    weight_terms = jnp.stack(partials).reshape(27 * channels, out_channels)
    grad_scale = 1.0 / math.sqrt(row_count * blk_count * grp_count)
    weight_grad = (lax.psum(weight_terms, ("grp", "blk")) * grad_scale).astype(jnp.bfloat16)
    weight_grad = weight_grad.reshape(27, channels, out_channels)
    returning = grad_grid[voxel_of_slot].reshape(blk_count, capacity, channels)
    returned = lax.all_to_all(returning, "blk", split_axis=0, concat_axis=0, tiled=True)
    grad_rows = returned.reshape(voxel_count, channels)[slot_index]
    return (output, grad_rows, weight_grad)


def fits(mesh):
    grp_count, blk_count = mesh.shape["grp"], mesh.shape["blk"]
    return blk_count == 16 and grp_count == 2


def solution(mesh):
    in_specs = (
        P(("grp", "blk"), None),
        P(("grp", "blk"), None),
        P(("grp", "blk"), None),
        P(),
        P("grp", "blk", None, None),
    )
    out_specs = (P("grp", "blk", None, None), P(("grp", "blk"), None), P())
    shards = gathered_shards if fits(mesh) else summed_shards
    return jax.shard_map(shards, mesh=mesh, in_specs=in_specs, out_specs=out_specs, check_vma=False)
```
